256 devices in a mesh: mp: 2 (over y_lo), vocab: 64 (over x, z, core), rows: 2 (over y_hi).
Axes of the slice: x: 4, y: 4 (y_hi: 2, y_lo: 2; y = y_hi * 2 + y_lo), z: 8, core: 2. Of those that a mesh axis runs over, the one named last changes fastest.
Arguments:
- hidden: bfloat16 [2, 512, 4096], P('mp', None, 'rows')
- norm_gain: bfloat16 [2, 4096], P('mp', 'rows'), may hold values from 0.5 to 1.5
- head_weights: bfloat16 [2, 4096, 98304], P('mp', 'rows', 'vocab')
- pair_source: int32 [256], P('vocab'), may hold values from 0 to 191, as said below
- pair_target: int32 [256], P('vocab'), may hold values from 0 to 191, as said below
- pair_count: int32 [64], P('vocab'), may hold values from 2 to 4, as said below
- pair_weight: bfloat16 [256, 512, 512], P('vocab'), may hold values from 0.00019454956 to 0.00390625
- next_token: int32 [512], P(('mp', 'rows')), may hold values from 0 to 98303
Outputs:
- ensemble_logp: float32 [512, 98304], P(('mp', 'rows'), 'vocab')
- target_nll: float32 [512], P(('mp', 'rows'))
The draws below stay inside these ranges and needn't reach their ends.
Inputs may be any that keep to these rules, and one draw needn't show every extreme that they name: `pair_target`: slot p targets one of the blocks of its own shard, (p // 4) * 3 to (p // 4) * 3 + 2. `pair_source`: slot p's source block lies from (p // 4) * 3 - 3 to (p // 4) * 3 + 2 * 3 - 1; slot 0 of every shard but the first and the last takes the block just below the shard's own, slot 1 of every shard but the last the block just above. The live slots of a shard are its first pair_count ones.
All inputs are finite; a program needn't handle non-finite values.
Results may differ from the reference program's by a relative error of at most 0.0003.
Values may be sent and summed in bfloat16 or wider, within the bound.
A program may use at most 128 MiB of HBM per device.

```python
import math
import jax
import jax.numpy as jnp
from jax import lax

D = 4096
BLOCK = 512
BLK_DEV = 3
SLOTS = 4
ROWS = 512
SHARDS = 64
VOCAB = 98304
NBLOCKS = 192
PAIRS = 256


def drawn_columns(key):
    aligned = min(8, ROWS)
    return jax.random.randint(jax.random.fold_in(key, 57), (2, aligned, 2), 0, VOCAB)


def raw_column(key, model_index, column):
    column_key = jax.random.fold_in(jax.random.fold_in(key, 31 + model_index), column)
    return jnp.clip(jax.random.normal(column_key, (D,), jnp.float32), -6.0, 6.0)


def head_column(key, model_index, column):
    chosen = drawn_columns(key)[model_index].reshape(-1)
    boost = jnp.where(jnp.any(chosen == column), max(1.5, 80.0 / math.sqrt(D)), 1.0)
    return raw_column(key, model_index, column) * (3.5 / math.sqrt(D)) * boost


def draw_head_weights(key, part):
    columns = jnp.arange(VOCAB, dtype=jnp.int32)
    llama_head = jax.vmap(lambda column: head_column(key, 0, column))(columns).T
    qwen_head = jax.vmap(lambda column: head_column(key, 1, column))(columns).T
    return jnp.stack([llama_head, qwen_head]).astype(jnp.bfloat16)


def draw_hidden(key, part):
    base_key = key
    key = jax.random.fold_in(key, 7)
    samples = jnp.clip(jax.random.normal(key, (2, ROWS, D), jnp.float32), -6.0, 6.0)
    aligned = min(8, ROWS)
    chosen = drawn_columns(base_key)
    strength = 1.0 - 0.05 * jnp.arange(aligned, dtype=jnp.float32)
    second = jnp.where(jnp.arange(aligned) % 2 == 0, 0.0, 1.0)
    for model_index in range(2):
        first_dir = jax.vmap(lambda column: raw_column(base_key, model_index, column))(chosen[model_index, :, 0])
        second_dir = jax.vmap(lambda column: raw_column(base_key, model_index, column))(chosen[model_index, :, 1])
        direction = first_dir + second[:, None] * second_dir
        rows_scale = jnp.sqrt(jnp.mean(samples[model_index, :aligned] ** 2, axis=1, keepdims=True))
        rows_new = strength[:, None] * direction * rows_scale + (1.0 - strength[:, None]) * samples[model_index, :aligned]
        samples = samples.at[model_index, :aligned].set(rows_new)
    return samples.astype(jnp.bfloat16)


def pair_lists(key):
    key = jax.random.fold_in(key, 101)
    sub_keys = jax.random.split(key, 5)
    device_index = jnp.arange(PAIRS, dtype=jnp.int32) // SLOTS
    slot_index = jnp.arange(PAIRS, dtype=jnp.int32) % SLOTS
    target = device_index * BLK_DEV + jax.random.randint(sub_keys[0], (PAIRS,), 0, BLK_DEV)
    lower_bound = jnp.maximum(device_index * BLK_DEV - BLK_DEV, 0)
    upper_bound = jnp.minimum(device_index * BLK_DEV + 2 * BLK_DEV, NBLOCKS)
    source = jax.random.randint(sub_keys[1], (PAIRS,), lower_bound, upper_bound)
    below = jnp.maximum(device_index * BLK_DEV - 1, 0)
    above = jnp.minimum(device_index * BLK_DEV + BLK_DEV, NBLOCKS - 1)
    source = jnp.where(slot_index == 0, below, jnp.where(slot_index == 1, above, source))
    first_slot = (device_index == 0) & (slot_index == 0)
    last_slot = (device_index == SHARDS - 1) & (slot_index == 0)
    source = jnp.where(first_slot, 0, jnp.where(last_slot, NBLOCKS - 1, source))
    target = jnp.where(first_slot, 0, jnp.where(last_slot, NBLOCKS - 1, target))
    counts = jax.random.randint(sub_keys[2], (SHARDS,), 2, SLOTS + 1)
    busiest = jax.random.randint(sub_keys[3], (), 0, SHARDS)
    lightest = (busiest + 1 + jax.random.randint(sub_keys[4], (), 0, SHARDS - 1)) % SHARDS
    shard_index = jnp.arange(SHARDS, dtype=jnp.int32)
    counts = jnp.where(shard_index == busiest, SLOTS, jnp.where(shard_index == lightest, 2, counts))
    return (source.astype(jnp.int32), target.astype(jnp.int32), counts.astype(jnp.int32))


def draw_pair_source(key, part):
    return pair_lists(key)[0]


def draw_pair_target(key, part):
    return pair_lists(key)[1]


def draw_pair_count(key, part):
    return pair_lists(key)[2]


def place_ends(values, stream_key, least, top_value):
    dims = values.shape
    spot = [jax.random.randint(jax.random.fold_in(stream_key, axis), (), 0, dims[axis]) for axis in range(len(dims))]
    values = values.at[tuple(spot)].set(least)
    longest = dims.index(max(dims))
    spot[longest] = (spot[longest] + 1) % dims[longest]
    return values.at[tuple(spot)].set(top_value)


def level_of(rng, dims, cuts, least, top_value):
    gain, own = 1.0, jax.random.fold_in(rng, 6)
    for axis_at, blocks in cuts:
        steps = jnp.exp(jax.random.uniform(jax.random.fold_in(own, axis_at), (blocks,), jnp.float32, least / len(cuts), top_value / len(cuts)))
        gain = gain * jnp.repeat(steps, dims[axis_at] // blocks).reshape([-1 if axis == axis_at else 1 for axis in range(len(dims))])
    return gain


def setup_inputs(seed: int = 0) -> dict:
    arg_keys = jax.random.split(jax.random.key(seed), 9)
    return {
        "hidden": draw_hidden(jax.random.fold_in(arg_keys[8], 71), 0),
        "norm_gain": jnp.clip(1.0 + 0.1 * jax.random.normal(arg_keys[1], (2, D), jnp.float32), 0.5, 1.5).astype(jnp.bfloat16),
        "head_weights": draw_head_weights(jax.random.fold_in(arg_keys[8], 71), 0),
        "pair_source": draw_pair_source(jax.random.fold_in(arg_keys[8], 71), 0),
        "pair_target": draw_pair_target(jax.random.fold_in(arg_keys[8], 71), 0),
        "pair_count": draw_pair_count(jax.random.fold_in(arg_keys[8], 71), 0),
        "pair_weight": jnp.clip(0.00019454956 + 0.0037117004 * jax.random.uniform(arg_keys[6], (PAIRS, BLOCK, BLOCK), jnp.float32) ** level_of(arg_keys[6], (PAIRS, BLOCK, BLOCK), ((0, 64),), -0.2, 0.2), 0.00019454956, 0.00390625).astype(jnp.bfloat16),
        "next_token": place_ends(jax.random.randint(arg_keys[7], (ROWS,), 0, VOCAB), jax.random.fold_in(arg_keys[7], 1), 0, VOCAB - 1).astype(jnp.int32),
    }


def reference(hidden, norm_gain, head_weights, pair_source, pair_target, pair_count, pair_weight, next_token):
    values = hidden.astype(jnp.float32)
    scale = lax.rsqrt(lax.optimization_barrier(jnp.mean(values * values, axis=2, keepdims=True)) + 1e-05)
    normed = values * scale * norm_gain.astype(jnp.float32)[:, None, :]
    llama_logits = jnp.dot(normed[0], head_weights[0].astype(jnp.float32), preferred_element_type=jnp.float32, precision=lax.Precision.HIGHEST)
    qwen_logits = jnp.dot(normed[1], head_weights[1].astype(jnp.float32), preferred_element_type=jnp.float32, precision=lax.Precision.HIGHEST)
    llama_peak = lax.optimization_barrier(jnp.max(llama_logits, axis=1, keepdims=True))
    llama_total = lax.optimization_barrier(jnp.sum(jnp.exp(llama_logits - llama_peak), axis=1, keepdims=True))
    llama_logp = llama_logits - llama_peak - jnp.log(llama_total)
    qwen_peak = lax.optimization_barrier(jnp.max(qwen_logits, axis=1, keepdims=True))
    qwen_total = lax.optimization_barrier(jnp.sum(jnp.exp(qwen_logits - qwen_peak), axis=1, keepdims=True))
    qwen_prob = (jnp.exp(qwen_logits - qwen_peak) / qwen_total).astype(jnp.bfloat16)
    blocks = qwen_prob.reshape(ROWS, NBLOCKS, BLOCK)
    picked_blocks = jnp.take(blocks, pair_source, axis=1).astype(jnp.float32)
    contribution = jnp.einsum('rpk,pkn->prn', picked_blocks, pair_weight.astype(jnp.float32), precision=lax.Precision.HIGHEST)
    slot_index = jnp.arange(PAIRS, dtype=jnp.int32) % SLOTS
    owner_index = jnp.arange(PAIRS, dtype=jnp.int32) // SLOTS
    live_slot = slot_index < pair_count[owner_index]
    selector = ((pair_target[:, None] == jnp.arange(NBLOCKS, dtype=jnp.int32)[None, :]) & live_slot[:, None]).astype(jnp.float32)
    mapped = jnp.einsum('prn,pb->rbn', contribution, selector, precision=lax.Precision.HIGHEST).reshape(ROWS, VOCAB)
    mixed = jnp.logaddexp(jnp.maximum(llama_logp, -50.0), jnp.log(mapped))
    log_norm = jnp.log1p(lax.optimization_barrier(jnp.sum(mapped, axis=1)))
    ensemble = mixed - log_norm[:, None]
    picked = jnp.take_along_axis(mixed, next_token[:, None], axis=1)[:, 0]
    return (ensemble, log_norm - picked)
```

```python
import functools

import jax
import jax.numpy as jnp
from jax import lax
from jax.experimental import pallas as pl
from jax.experimental.pallas import tpu as pltpu
from jax.sharding import PartitionSpec as P

MESH = pl.DeviceIdType.MESH
NX, NZ, NC = 4, 8, 2
Q = 128
CW = 256
BLOCK = 512
NCH = 6
NB = 3
FEAT = 2048
FLOOR = 1.9287498479639178e-22


def kernel(
    hid, gain, head, psrc, ptgt, pcnt, wts, ntok,
    out, nll,
    xraw, x2, g_buf, hb, wb, snd, sndm, rcv, rcvm, own, el, ql, pq, pm, mp_buf, st, part_st, all_st,
    ld_sem, hd_sem, ys, yr, yms, ymr, hs, hr, hms, hmr, cs, as_, ar,
):
    m = lax.axis_index("mp")
    v = lax.axis_index("vocab")
    r = lax.axis_index("rows")
    x, z, c = v // (NZ * NC), lax.rem(v // NC, NZ), lax.rem(v, NC)
    v_up, v_down = lax.rem(v + 1, 64), lax.rem(v + 63, 64)

    peers = [(1 - m, v, r), (1 - m, v, 1 - r), (m, v, 1 - r)]
    quarters = [(1 - m) * 2 + r, (1 - m) * 2 + 1 - r, m * 2 + 1 - r, m * 2 + r]
    core_peer = (m, (x * NZ + z) * NC + 1 - c, r)

    def far(dx, dz):
        return (m, (lax.rem(x + dx, NX) * NZ + lax.rem(z + dz, NZ)) * NC + c, r)

    offsets = [(dx, dz) for dx in range(NX) for dz in range(NZ) if dx or dz]

    c_hid = pltpu.make_async_copy(hid.at[0], xraw, ld_sem.at[0])
    c_gain = pltpu.make_async_copy(gain, g_buf, ld_sem.at[1])
    c_w = pltpu.make_async_copy(wts, wb, ld_sem.at[2])
    c_hid.start()
    c_gain.start()

    def head_copy(j):
        cols = pl.ds(pl.multiple_of(j * CW, CW), CW)
        return pltpu.make_async_copy(head.at[0, :, cols], hb.at[j], hd_sem.at[j])

    for j in range(NCH):
        head_copy(j).start()
    c_w.start()

    barrier = pltpu.get_barrier_semaphore()
    greet = peers + [(m, v_up, r), (m, v_down, r)] + [far(*o) for o in offsets]
    for d in greet:
        pl.semaphore_signal(barrier, inc=1, device_id=d, device_id_type=MESH)

    rows_i = lax.broadcasted_iota(jnp.int32, (Q, Q), 0)
    cols_i = lax.broadcasted_iota(jnp.int32, (Q, Q), 1)
    eye = rows_i == cols_i

    def to_row(col):
        return jnp.sum(jnp.where(eye, col, 0.0), axis=0, keepdims=True)

    def to_col(row):
        return jnp.sum(jnp.where(eye, row, 0.0), axis=1, keepdims=True)

    c_hid.wait()
    c_gain.wait()
    g = g_buf[...].astype(jnp.float32)
    for k in range(4):
        a = xraw[pl.ds(pl.multiple_of(quarters[k] * Q, Q), Q), :].astype(jnp.float32)
        sq = jnp.sum(a * a, axis=1, keepdims=True)
        if k < 3:
            for j in range(NCH):
                sndm[j, k, 1:2, :] = to_row(sq)
        else:
            own_sq = sq
        a = a * g
        hi = a.astype(jnp.bfloat16)
        x2[k * 2 * Q : k * 2 * Q + Q, :] = hi
        x2[k * 2 * Q + Q : (k + 1) * 2 * Q, :] = (a - hi.astype(jnp.float32)).astype(jnp.bfloat16)

    pl.semaphore_wait(barrier, len(greet))

    def y_copy(j, k):
        return pltpu.make_async_remote_copy(
            src_ref=snd.at[j, k], dst_ref=rcv.at[j, k], send_sem=ys.at[j, k], recv_sem=yr.at[j, k],
            device_id=peers[k], device_id_type=MESH,
        )

    def ym_copy(j, k):
        return pltpu.make_async_remote_copy(
            src_ref=sndm.at[j, k], dst_ref=rcvm.at[j, k], send_sem=yms.at[j, k], recv_sem=ymr.at[j, k],
            device_id=peers[k], device_id_type=MESH,
        )

    def produce(j, carry):
        head_copy(j).wait()
        w = hb[j]
        for k in range(4):
            p2 = jnp.dot(x2[k * 2 * Q : (k + 1) * 2 * Q, :], w, preferred_element_type=jnp.float32)
            p = p2[:Q] + p2[Q:]
            if k == 3:
                own[j] = p
            else:
                top = jnp.maximum(jnp.max(jnp.abs(p), axis=1, keepdims=True), 1e-30)
                snd[j, k] = jnp.round(p * (32767.0 / top)).astype(jnp.int32).astype(jnp.int16)
                y_copy(j, k).start()
                sndm[j, k, 0:1, :] = to_row(top * (1.0 / 32767.0))
                ym_copy(j, k).start()
        return carry

    lax.fori_loop(0, NCH, produce, 0)

    def halo(b):
        copies = []
        for d, (target, slot) in enumerate((((m, v_up, r), b), ((m, v_down, r), 2 * NB + b))):
            copies.append(pltpu.make_async_remote_copy(
                src_ref=pq.at[NB + b], dst_ref=pq.at[slot], send_sem=hs.at[d, b], recv_sem=hr.at[d, b],
                device_id=target, device_id_type=MESH,
            ))
            copies.append(pltpu.make_async_remote_copy(
                src_ref=pm.at[NB + b], dst_ref=pm.at[slot], send_sem=hms.at[d, b], recv_sem=hmr.at[d, b],
                device_id=target, device_id_type=MESH,
            ))
        return copies

    token = to_col(ntok[...].astype(jnp.float32))
    lane = lax.broadcasted_iota(jnp.int32, (Q, BLOCK), 1).astype(jnp.float32)
    scale_own = scale_oth = None
    l_tops, q_tops, l_sums, q_sums = [], [], [], []
    tok_l = jnp.zeros((Q, 1), jnp.float32)
    for b in range(NB):
        for j in (2 * b, 2 * b + 1):
            for k in range(3):
                y_copy(j, k).wait_recv()
                ym_copy(j, k).wait_recv()
            if j == 0:
                sq = [to_col(rcvm[0, k, 1:2, :]) for k in range(3)]
                scale_own = lax.rsqrt((own_sq + sq[2]) * (1.0 / 4096.0) + 1e-05)
                scale_oth = lax.rsqrt((sq[0] + sq[1]) * (1.0 / 4096.0) + 1e-05)
            f = [to_col(rcvm[j, k, 0:1, :]) for k in range(3)]
            half = slice((j % 2) * CW, (j % 2 + 1) * CW)
            mine = own[j] * scale_own + rcv[j, 2].astype(jnp.float32) * (f[2] * scale_own)
            other = rcv[j, 0].astype(jnp.float32) * (f[0] * scale_oth) + rcv[j, 1].astype(
                jnp.float32
            ) * (f[1] * scale_oth)
            ql[m, :, half] = mine
            ql[1 - m, :, half] = other
        qb = ql[1]
        top = jnp.max(qb, axis=1, keepdims=True)
        e = jnp.exp(qb - top)
        pq[NB + b] = e.astype(jnp.bfloat16)
        pm[NB + b] = to_row(top)
        for cp in halo(b):
            cp.start()
        q_tops.append(top)
        q_sums.append(jnp.sum(e, axis=1, keepdims=True))
        lb = ql[0]
        top = jnp.max(lb, axis=1, keepdims=True)
        e = jnp.exp(lb - top)
        el[b] = e
        l_tops.append(top)
        l_sums.append(jnp.sum(e, axis=1, keepdims=True))
        base = ((v * NB + b) * BLOCK).astype(jnp.float32)
        tok_l = tok_l + jnp.sum(jnp.where(lane == token - base, lb, 0.0), axis=1, keepdims=True)

    def combine(tops, sums):
        top = functools.reduce(jnp.maximum, tops)
        return top, sum(s * jnp.exp(t - top) for s, t in zip(sums, tops))

    l_top, l_sum = combine(l_tops, l_sums)
    q_top, q_sum = combine(q_tops, q_sums)

    c_w.wait()
    for b in range(NB):
        for cp in halo(b):
            cp.wait_recv()

    live, target, tops, prods = [], [], [], []
    for s in range(4):
        at = jnp.clip(psrc[s] - (v * NB - NB), 0, 3 * NB - 1)
        alive = (pcnt[0] > s).astype(jnp.float32)
        live.append(alive)
        target.append(ptgt[s] - v * NB)
        tops.append(to_col(pm[at]))
        prods.append(jnp.dot(pq[at], wb[s], preferred_element_type=jnp.float32))
    shift = functools.reduce(
        jnp.maximum, [jnp.where(a > 0.5, t, -jnp.inf) for a, t in zip(live, tops)]
    )
    factors = [
        jnp.where(a > 0.5, jnp.exp(jnp.minimum(t - shift, 0.0)), 0.0) for a, t in zip(live, tops)
    ]
    mass = jnp.zeros((Q, 1), jnp.float32)
    tok_m = jnp.zeros((Q, 1), jnp.float32)
    for t in range(NB):
        total = sum(
            prods[s] * (factors[s] * (target[s] == t).astype(jnp.float32)) for s in range(4)
        )
        mp_buf[t] = total
        mass = mass + jnp.sum(total, axis=1, keepdims=True)
        base = ((v * NB + t) * BLOCK).astype(jnp.float32)
        tok_m = tok_m + jnp.sum(jnp.where(lane == token - base, total, 0.0), axis=1, keepdims=True)

    t_top = jnp.maximum(q_top, shift)
    up = jnp.exp(shift - t_top)
    for i, col in enumerate(
        (t_top, q_sum * jnp.exp(q_top - t_top), mass * up, tok_m * up, l_top, l_sum, tok_l)
    ):
        st[i : i + 1, :] = to_row(col)
    st[7:8, :] = jnp.zeros((1, Q), jnp.float32)

    def merge(rows):
        tq, tl = rows[0], rows[4]
        nq = jnp.max(tq, axis=0, keepdims=True)
        nl = jnp.max(tl, axis=0, keepdims=True)
        eq, e_l = jnp.exp(tq - nq), jnp.exp(tl - nl)

        def add(a):
            return jnp.sum(a, axis=0, keepdims=True)

        return (
            nq, add(rows[1] * eq), add(rows[2] * eq), add(rows[3] * eq), nl, add(rows[5] * e_l), add(rows[6]),
        )

    core = pltpu.make_async_remote_copy(
        src_ref=st, dst_ref=part_st, send_sem=cs.at[0], recv_sem=cs.at[1],
        device_id=core_peer, device_id_type=MESH,
    )
    core.start()
    core.wait_recv()
    pair = [jnp.concatenate([st[i : i + 1, :], part_st[i : i + 1, :]], axis=0) for i in range(7)]
    for i, row in enumerate(merge(pair)):
        all_st[0, i : i + 1, :] = row
    all_st[0, 7:8, :] = jnp.zeros((1, Q), jnp.float32)

    spread = [
        pltpu.make_async_remote_copy(
            src_ref=all_st.at[0], dst_ref=all_st.at[dx * NZ + dz], send_sem=as_.at[dx * NZ + dz],
            recv_sem=ar.at[dx * NZ + dz], device_id=far(dx, dz), device_id_type=MESH,
        )
        for dx, dz in offsets
    ]
    for cp in spread:
        cp.start()
    for cp in spread:
        cp.wait_recv()
    nq, sum_q, sum_m, sum_t, nl, sum_l, t_l = merge([all_st[:, i, :] for i in range(7)])
    lse_l = nl + jnp.log(sum_l)
    log_norm = jnp.log(1.0 + sum_m / sum_q)
    nll[...] = log_norm - jnp.log(
        jnp.maximum(jnp.exp(t_l - lse_l), FLOOR) + sum_t / sum_q
    )
    lse_col = to_col(lse_l)
    norm_col = to_col(log_norm)
    m_fac = jnp.exp(shift - to_col(nq)) / to_col(sum_q)
    for b in range(NB):
        l_fac = jnp.exp(l_tops[b] - lse_col)
        out[:, b * BLOCK : (b + 1) * BLOCK] = (
            jnp.log(jnp.maximum(el[b] * l_fac, FLOOR) + mp_buf[b] * m_fac) - norm_col
        )

    for j in range(NCH):
        for k in range(3):
            y_copy(j, k).wait_send()
            ym_copy(j, k).wait_send()
    for b in range(NB):
        for cp in halo(b):
            cp.wait_send()
    core.wait_send()
    for cp in spread:
        cp.wait_send()


def on_device(
    hidden, norm_gain, head_weights, pair_source, pair_target, pair_count, pair_weight, next_token
):
    hbm = pl.BlockSpec(memory_space=pl.ANY)
    smem = pl.BlockSpec(memory_space=pltpu.SMEM)
    vmem = pl.BlockSpec(memory_space=pltpu.VMEM)
    dma = pltpu.SemaphoreType.DMA
    f32, bf16 = jnp.float32, jnp.bfloat16
    ensemble, nll = pl.pallas_call(
        kernel,
        out_shape=(
            jax.ShapeDtypeStruct((Q, NB * BLOCK), f32),
            jax.ShapeDtypeStruct((1, Q), f32),
        ),
        in_specs=[hbm, hbm, hbm, smem, smem, smem, hbm, vmem],
        out_specs=(vmem, vmem),
        scratch_shapes=[
            pltpu.VMEM((4 * Q, FEAT), bf16),
            pltpu.VMEM((8 * Q, FEAT), bf16),
            pltpu.VMEM((1, FEAT), bf16),
            pltpu.VMEM((NCH, FEAT, CW), bf16),
            pltpu.VMEM((4, BLOCK, BLOCK), bf16),
            pltpu.VMEM((NCH, 3, Q, CW), jnp.int16),
            pltpu.VMEM((NCH, 3, 2, Q), f32),
            pltpu.VMEM((NCH, 3, Q, CW), jnp.int16),
            pltpu.VMEM((NCH, 3, 2, Q), f32),
            pltpu.VMEM((NCH, Q, CW), f32),
            pltpu.VMEM((NB, Q, BLOCK), f32),
            pltpu.VMEM((2, Q, BLOCK), f32),
            pltpu.VMEM((3 * NB, Q, BLOCK), bf16),
            pltpu.VMEM((3 * NB, 1, Q), f32),
            pltpu.VMEM((NB, Q, BLOCK), f32),
            pltpu.VMEM((8, Q), f32),
            pltpu.VMEM((8, Q), f32),
            pltpu.VMEM((NX * NZ, 8, Q), f32),
            dma((3,)),
            dma((NCH,)),
            dma((NCH, 3)),
            dma((NCH, 3)),
            dma((NCH, 3)),
            dma((NCH, 3)),
            dma((2, NB)),
            dma((2, NB)),
            dma((2, NB)),
            dma((2, NB)),
            dma((2,)),
            dma((NX * NZ,)),
            dma((NX * NZ,)),
        ],
        compiler_params=pltpu.CompilerParams(
            collective_id=0, has_side_effects=True, vmem_limit_bytes=48 * 2**20
        ),
        cost_estimate=pl.CostEstimate(
            flops=4 * 4 * Q * FEAT * NB * BLOCK, bytes_accessed=12 * 2**20, transcendentals=10**6
        ),
        name="ensemble",
    )(
        hidden, norm_gain, head_weights, pair_source, pair_target, pair_count, pair_weight,
        next_token.reshape(1, Q),
    )
    return ensemble, nll.reshape(Q)


def solution(mesh):
    in_specs = (
        P("mp", None, "rows"),
        P("mp", "rows"),
        P("mp", "rows", "vocab"),
        P("vocab"),
        P("vocab"),
        P("vocab"),
        P("vocab", None, None),
        P(("mp", "rows")),
    )
    out_specs = (P(("mp", "rows"), "vocab"), P(("mp", "rows")))
    return jax.shard_map(
        on_device, mesh=mesh, in_specs=in_specs, out_specs=out_specs, check_vma=False
    )
```

```python
import functools

import jax
import jax.numpy as jnp
from jax import lax
from jax.experimental import pallas as pl
from jax.experimental.pallas import tpu as pltpu
from jax.sharding import PartitionSpec as P

MESH = pl.DeviceIdType.MESH
NX, NZ, NC = 4, 8, 2
Q = 128
CW = 256
BLOCK = 512
NCH = 6
NB = 3
FEAT = 2048
FLOOR = 1.9287498479639178e-22


def kernel(
    hid, gain, head, psrc_in, ptgt_in, pcnt_in, wts, ntok_in,
    out, nll,
    psrc, ptgt, pcnt, ntok, xraw, x2, g_buf, hb, wb, snd, sndm, part, rcv, rcvm, own, own_sq, lg, el, pq, pm, q_sums,
    l_tops, l_lse, l_tok, mp_buf, st_q, got_q, all_q, st_l, got_l, all_l,
    ld_sem, hd_sem, ys, yr, yms, ymr, hs, hr, hms, hmr, cs, qss, qsr, lss, lsr,
):
    m = lax.axis_index("mp")
    v = lax.axis_index("vocab")
    r = lax.axis_index("rows")
    x, z, c = v // (NZ * NC), lax.rem(v // NC, NZ), lax.rem(v, NC)
    v_up, v_down = lax.rem(v + 1, 64), lax.rem(v + 63, 64)

    peers = [(1 - m, v, r), (1 - m, v, 1 - r), (m, v, 1 - r)]
    quarters = [(1 - m) * 2 + r, (1 - m) * 2 + 1 - r, m * 2 + 1 - r, m * 2 + r]
    core_peer = (m, (x * NZ + z) * NC + 1 - c, r)

    def far(dx, dz):
        return (m, (lax.rem(x + dx, NX) * NZ + lax.rem(z + dz, NZ)) * NC + c, r)

    offsets = sorted(
        ((dx, dz) for dx in range(NX) for dz in range(NZ) if dx or dz),
        key=lambda o: -min(o[0], NX - o[0]) - min(o[1], NZ - o[1]),
    )

    c_hid = pltpu.make_async_copy(hid.at[0], xraw, ld_sem.at[0])
    c_gain = pltpu.make_async_copy(gain, g_buf, ld_sem.at[1])
    c_w = pltpu.make_async_copy(wts, wb, ld_sem.at[2])
    c_hid.start()
    c_gain.start()

    def head_copy(j):
        cols = pl.ds(pl.multiple_of(j * CW, CW), CW)
        return pltpu.make_async_copy(head.at[0, :, cols], hb.at[j], hd_sem.at[j])

    for j in range(NCH):
        head_copy(j).start()
    c_w.start()
    lists = [
        pltpu.make_async_copy(src, dst, ld_sem.at[3 + i])
        for i, (src, dst) in enumerate(
            ((psrc_in, psrc), (ptgt_in, ptgt), (pcnt_in, pcnt), (ntok_in, ntok))
        )
    ]
    for cp in lists:
        cp.start()

    barrier = pltpu.get_barrier_semaphore()
    greet = peers + [(m, v_up, r), (m, v_down, r)] + [far(*o) for o in offsets]
    for d in greet:
        pl.semaphore_signal(barrier, inc=1, device_id=d, device_id_type=MESH)

    rows_i = lax.broadcasted_iota(jnp.int32, (Q, Q), 0)
    cols_i = lax.broadcasted_iota(jnp.int32, (Q, Q), 1)
    eye = rows_i == cols_i

    def to_row(col):
        return jnp.sum(jnp.where(eye, col, 0.0), axis=0, keepdims=True)

    def to_col(row):
        return jnp.sum(jnp.where(eye, row, 0.0), axis=1, keepdims=True)

    for edge, at in ((v == 0, 0), (v == 63, 2 * NCH)):

        @pl.when(edge)
        def _(at=at):
            pq[at : at + NCH] = jnp.zeros((NCH, Q, CW), jnp.bfloat16)
            pm[at : at + NCH] = jnp.zeros((NCH, 1, Q), jnp.float32)

    c_hid.wait()
    c_gain.wait()
    g = g_buf[...].astype(jnp.float32)
    for k in range(4):
        a = xraw[pl.ds(pl.multiple_of(quarters[k] * Q, Q), Q), :].astype(jnp.float32)
        sq = jnp.sum(a * a, axis=1, keepdims=True)
        if k < 3:
            for j in range(NCH):
                sndm[j, k, 1:2, :] = to_row(sq)
        else:
            own_sq = sq
        a = a * g
        hi = a.astype(jnp.bfloat16)
        x2[k * 2 * Q : k * 2 * Q + Q, :] = hi
        x2[k * 2 * Q + Q : (k + 1) * 2 * Q, :] = (a - hi.astype(jnp.float32)).astype(jnp.bfloat16)

    pl.semaphore_wait(barrier, len(greet))

    def y_copy(j, k):
        return pltpu.make_async_remote_copy(
            src_ref=snd.at[j, k], dst_ref=rcv.at[j, k], send_sem=ys, recv_sem=yr.at[j],
            device_id=peers[k], device_id_type=MESH,
        )

    def ym_copy(j, k):
        return pltpu.make_async_remote_copy(
            src_ref=sndm.at[j, k], dst_ref=rcvm.at[j, k], send_sem=yms, recv_sem=ymr.at[j],
            device_id=peers[k], device_id_type=MESH,
        )

    def multiply(j):
        head_copy(j).wait()
        w = hb[j]
        for k in range(4):
            p2 = jnp.dot(x2[k * 2 * Q : (k + 1) * 2 * Q, :], w, preferred_element_type=jnp.float32)
            p = p2[:Q] + p2[Q:]
            if k == 3:
                own[j] = p
            else:
                part[j % 2, k] = p

    def pack(j):
        for k in range(3):
            p = part[j % 2, k]
            top = jnp.maximum(jnp.max(jnp.abs(p), axis=1, keepdims=True), 1e-30)
            snd[j, k] = jnp.round(p * (32767.0 / top)).astype(jnp.int32).astype(jnp.int16)
            sndm[j, k, 0:1, :] = to_row(top * (1.0 / 32767.0))

    def send(j):
        for k in range(3):
            y_copy(j, k).start()
            ym_copy(j, k).start()

    def wait_all(ref, sem):
        pltpu.make_async_copy(ref, ref, sem).wait()

    multiply(0)
    pack(0)
    send(0)
    for j in range(1, NCH + 1):
        if j < NCH:
            multiply(j)
        if j > 1:
            pack(j - 1)
            send(j - 1)

    has = (v < 63, v > 0)

    def halo(j, d):
        target, slot = (((m, v_up, r), j), ((m, v_down, r), 2 * NCH + j))[d]
        return [
            pltpu.make_async_remote_copy(
                src_ref=buf.at[NCH + j], dst_ref=buf.at[slot], send_sem=send.at[d], recv_sem=recv.at[d],
                device_id=target, device_id_type=MESH,
            )
            for buf, send, recv in ((pq, hs, hr), (pm, hms, hmr))
        ]

    def halo_start(j):
        for d in range(2):

            @pl.when(has[d])
            def _(d=d):
                for cp in halo(j, d):
                    cp.start()

    for cp in lists:
        cp.wait()
    token = to_col(ntok[...].reshape(1, Q).astype(jnp.float32))
    lane = lax.broadcasted_iota(jnp.int32, (Q, BLOCK), 1).astype(jnp.float32)

    def at_token(start, values):
        base = (v * (NB * BLOCK) + start).astype(jnp.float32)
        hit = lane[:, : values.shape[1]] == token - base
        return jnp.sum(jnp.where(hit, values, 0.0), axis=1, keepdims=True)

    scale_own = scale_other = None
    for j in range(NCH):
        wait_all(rcv.at[j], yr.at[j])
        wait_all(rcvm.at[j], ymr.at[j])
        if j == 0:
            sq = [rcvm[0, k, 1:2, :] for k in range(3)]
            scale_own = lax.rsqrt((own_sq[...] + sq[2]) * (1.0 / 4096.0) + 1e-05)
            scale_other = lax.rsqrt((sq[0] + sq[1]) * (1.0 / 4096.0) + 1e-05)
        near, cross, far_term = (
            rcv[j, k].astype(jnp.float32)
            * to_col(rcvm[j, k, 0:1, :] * (scale_own if k == 2 else scale_other))
            for k in range(3)
        )
        lg[m] = own[j] * to_col(scale_own) + far_term
        lg[1 - m] = near + cross
        logits = lg[1]
        top = jnp.max(logits, axis=1, keepdims=True)
        e = jnp.exp(logits - top)
        pq[NCH + j] = e.astype(jnp.bfloat16)
        pm[NCH + j] = to_row(top)
        halo_start(j)
        q_sums[j] = to_row(jnp.sum(e, axis=1, keepdims=True))
        logits = lg[0]
        top = jnp.max(logits, axis=1, keepdims=True)
        e = jnp.exp(logits - top)
        el[j] = e
        l_tops[j] = to_row(top)
        l_lse[j] = to_row(top + jnp.log(jnp.sum(e, axis=1, keepdims=True)))
        l_tok[j] = to_row(at_token(j * CW, logits))

    def add(a):
        return jnp.sum(a, axis=0, keepdims=True)

    def merge_q(top, *sums):
        new = jnp.max(top, axis=0, keepdims=True)
        e = jnp.exp(top - new)
        return (new, *(add(a * e) for a in sums))

    def merge_l(lse, tok):
        new = jnp.max(lse, axis=0, keepdims=True)
        return new + jnp.log(add(jnp.exp(lse - new))), add(tok)

    def core_copy(src, dst, i):
        return pltpu.make_async_remote_copy(
            src_ref=src, dst_ref=dst, send_sem=cs.at[i], recv_sem=cs.at[i + 1],
            device_id=core_peer, device_id_type=MESH,
        )

    def spread(ref, send, recv):
        return [
            pltpu.make_async_remote_copy(
                src_ref=ref.at[0], dst_ref=ref.at[dx * NZ + dz], send_sem=send,
                recv_sem=recv, device_id=far(dx, dz), device_id_type=MESH,
            )
            for dx, dz in offsets
        ]

    def both(a, b, i):
        return jnp.concatenate([a[i : i + 1, :], b[i : i + 1, :]], axis=0)

    for i, row in enumerate(merge_l(
        jnp.concatenate([l_lse[j] for j in range(NCH)], axis=0),
        jnp.concatenate([l_tok[j] for j in range(NCH)], axis=0),
    )):
        st_l[i : i + 1, :] = row
    core_l = core_copy(st_l, got_l, 2)
    core_l.start()
    core_l.wait_recv()
    for i, row in enumerate(merge_l(*(both(st_l, got_l, i) for i in range(2)))):
        all_l[0, i : i + 1, :] = row
    spread_l = spread(all_l, lss, lsr)
    for cp in spread_l:
        cp.start()
    c_w.wait()

    for d in range(2):

        @pl.when(has[1 - d])
        def _(d=d):
            slots = pl.ds(2 * NCH * d, NCH)
            wait_all(pq.at[slots], hr.at[d])
            wait_all(pm.at[slots], hmr.at[d])


    live, target, tops, prods = [], [], [], []
    for s in range(4):
        at = 2 * jnp.clip(psrc[s] - (v * NB - NB), 0, 3 * NB - 1)
        for h in range(2):
            live.append((pcnt[0] > s).astype(jnp.float32))
            target.append(ptgt[s] - v * NB)
            tops.append(pm[at + h])
            prods.append(jnp.dot(
                pq[at + h], wb[s, h * CW : (h + 1) * CW, :], preferred_element_type=jnp.float32
            ))
    shift = functools.reduce(
        jnp.maximum, [jnp.where(a > 0.5, t, -jnp.inf) for a, t in zip(live, tops)]
    )
    factors = [
        to_col(jnp.where(a > 0.5, jnp.exp(jnp.minimum(t - shift, 0.0)), 0.0))
        for a, t in zip(live, tops)
    ]
    mass = jnp.zeros((Q, 1), jnp.float32)
    tok_m = jnp.zeros((Q, 1), jnp.float32)
    for t in range(NB):
        total = sum(
            prods[s] * (factors[s] * (target[s] == t).astype(jnp.float32)) for s in range(8)
        )
        mp_buf[t] = total
        mass = mass + jnp.sum(total, axis=1, keepdims=True)
        tok_m = tok_m + at_token(t * BLOCK, total)

    top, q_sum = merge_q(
        jnp.concatenate([pm[NCH + j] for j in range(NCH)], axis=0),
        jnp.concatenate([q_sums[j] for j in range(NCH)], axis=0),
    )
    t_top = jnp.maximum(top, shift)
    up = jnp.exp(shift - t_top)
    for i, row in enumerate((t_top, q_sum * jnp.exp(top - t_top), to_row(mass) * up, to_row(tok_m) * up)):
        st_q[i : i + 1, :] = row
    core_q = core_copy(st_q, got_q, 0)
    core_q.start()
    core_q.wait_recv()
    for i, row in enumerate(merge_q(*(both(st_q, got_q, i) for i in range(4)))):
        all_q[0, i : i + 1, :] = row
    spread_q = spread(all_q, qss, qsr)
    for cp in spread_q:
        cp.start()

    wait_all(snd, ys)
    wait_all(sndm, yms)
    for d in range(2):

        @pl.when(has[d])
        def _(d=d):
            wait_all(pq.at[pl.ds(NCH, NCH)], hs.at[d])
            wait_all(pm.at[pl.ds(NCH, NCH)], hms.at[d])

    core_q.wait_send()
    core_l.wait_send()
    others = pl.ds(1, NX * NZ - 1)
    wait_all(all_q.at[others], qss)
    wait_all(all_l.at[others], lss)
    wait_all(all_q.at[others], qsr)
    nq, sum_q, sum_m, sum_t = merge_q(*(all_q[:, i, :] for i in range(4)))
    log_norm = jnp.log(1.0 + sum_m / sum_q)
    norm_col = to_col(log_norm)
    m_fac = to_col(jnp.exp(shift - nq) / sum_q)
    wait_all(all_l.at[others], lsr)
    lse_l, t_l = merge_l(*(all_l[:, i, :] for i in range(2)))
    nll[...] = log_norm - jnp.log(jnp.maximum(jnp.exp(t_l - lse_l), FLOOR) + sum_t / sum_q)
    for j in range(NCH):
        l_fac = to_col(jnp.exp(l_tops[j] - lse_l))
        mapped = mp_buf[j // 2, :, (j % 2) * CW : (j % 2 + 1) * CW]
        out[:, j * CW : (j + 1) * CW] = (
            jnp.log(jnp.maximum(el[j] * l_fac, FLOOR) + mapped * m_fac) - norm_col
        )


def on_device(
    hidden, norm_gain, head_weights, pair_source, pair_target, pair_count, pair_weight, next_token
):
    hbm = pl.BlockSpec(memory_space=pltpu.HBM)
    vmem = pl.BlockSpec(memory_space=pltpu.VMEM)
    dma = pltpu.SemaphoreType.DMA
    f32, bf16 = jnp.float32, jnp.bfloat16
    ensemble, nll = pl.pallas_call(
        kernel,
        out_shape=(
            pltpu.VMEM((Q, NB * BLOCK), f32),
            pltpu.VMEM((1, Q), f32),
        ),
        in_specs=[pl.BlockSpec(memory_space=pl.ANY)] * 8,
        out_specs=(vmem, vmem),
        scratch_shapes=[
            pltpu.SMEM((4,), jnp.int32),
            pltpu.SMEM((4,), jnp.int32),
            pltpu.SMEM((1,), jnp.int32),
            pltpu.VMEM((Q,), jnp.int32),
            pltpu.VMEM((4 * Q, FEAT), bf16),
            pltpu.VMEM((8 * Q, FEAT), bf16),
            pltpu.VMEM((1, FEAT), bf16),
            pltpu.VMEM((NCH, FEAT, CW), bf16),
            pltpu.VMEM((4, BLOCK, BLOCK), bf16),
            pltpu.VMEM((NCH, 3, Q, CW), jnp.int16),
            pltpu.VMEM((NCH, 3, 2, Q), f32),
            pltpu.VMEM((2, 3, Q, CW), f32),
            pltpu.VMEM((NCH, 3, Q, CW), jnp.int16),
            pltpu.VMEM((NCH, 3, 2, Q), f32),
            pltpu.VMEM((NCH, Q, CW), f32),
            pltpu.VMEM((1, Q), f32),
            pltpu.VMEM((2, Q, CW), f32),
            pltpu.VMEM((NCH, Q, CW), f32),
            pltpu.VMEM((3 * NCH, Q, CW), bf16),
            pltpu.VMEM((3 * NCH, 1, Q), f32),
            pltpu.VMEM((NCH, 1, Q), f32),
            pltpu.VMEM((NCH, 1, Q), f32),
            pltpu.VMEM((NCH, 1, Q), f32),
            pltpu.VMEM((NCH, 1, Q), f32),
            pltpu.VMEM((NB, Q, BLOCK), f32),
            pltpu.VMEM((4, Q), f32),
            pltpu.VMEM((4, Q), f32),
            pltpu.VMEM((NX * NZ, 4, Q), f32),
            pltpu.VMEM((2, Q), f32),
            pltpu.VMEM((2, Q), f32),
            pltpu.VMEM((NX * NZ, 2, Q), f32),
            dma((7,)),
            dma((NCH,)),
            dma(()),
            dma((NCH,)),
            dma(()),
            dma((NCH,)),
            dma((2,)),
            dma((2,)),
            dma((2,)),
            dma((2,)),
            dma((4,)),
            dma(()),
            dma(()),
            dma(()),
            dma(()),
        ],
        compiler_params=pltpu.CompilerParams(
            collective_id=0, has_side_effects=True, vmem_limit_bytes=40 * 2**20
        ),
        cost_estimate=pl.CostEstimate(
            flops=4 * 4 * Q * FEAT * NB * BLOCK, bytes_accessed=12 * 2**20, transcendentals=10**6
        ),
        name="ensemble",
    )(
        *(a if a.shape == (1,) else pltpu.with_memory_space_constraint(a, pltpu.HBM) for a in (
            hidden, norm_gain, head_weights, pair_source, pair_target, pair_count, pair_weight,
            next_token,
        ))
    )
    return ensemble, nll.reshape(Q)


def solution(mesh):
    in_specs = (
        P("mp", None, "rows"),
        P("mp", "rows"),
        P("mp", "rows", "vocab"),
        P("vocab"),
        P("vocab"),
        P("vocab"),
        P("vocab", None, None),
        P(("mp", "rows")),
    )
    out_specs = (P(("mp", "rows"), "vocab"), P(("mp", "rows")))
    return jax.shard_map(
        on_device, mesh=mesh, in_specs=in_specs, out_specs=out_specs, check_vma=False
    )
```

```python
import functools

import jax
import jax.numpy as jnp
from jax import lax
from jax.experimental import pallas as pl
from jax.experimental.pallas import tpu as pltpu
from jax.sharding import PartitionSpec as P

MESH = pl.DeviceIdType.MESH
NX, NZ, NC = 4, 8, 2
Q = 128
CW = 256
BLOCK = 512
NCH = 6
NB = 3
FEAT = 2048
FLOOR = 1.9287498479639178e-22


def kernel(
    hid, gain, head, psrc_in, ptgt_in, pcnt_in, wts, ntok_in,
    el, mp_buf, l_fac, m_fac, norm_out, nll,
    psrc, ptgt, pcnt, ntok, xraw, x2, g_buf, hb, wb, snd, sndm, part, rcv, rcvm, own, own_sq, lg, pq, pm, q_sums,
    l_tops, l_lse, l_tok, st_q, got_q, all_q, all_t, st_l, got_l, all_l,
    ld_sem, hid_sem, hd_sem, ys, yr, yms, ymr, hs, hr, hms, hmr, cs, qss, qsr, lss, lsr, tss, tsr,
):
    m = lax.axis_index("mp")
    v = lax.axis_index("vocab")
    r = lax.axis_index("rows")
    x, z, c = v // (NZ * NC), lax.rem(v // NC, NZ), lax.rem(v, NC)
    v_up, v_down = lax.rem(v + 1, 64), lax.rem(v + 63, 64)

    peers = [(1 - m, v, r), (1 - m, v, 1 - r), (m, v, 1 - r)]
    quarters = [(1 - m) * 2 + r, (1 - m) * 2 + 1 - r, m * 2 + 1 - r, m * 2 + r]
    core_peer = (m, (x * NZ + z) * NC + 1 - c, r)

    def far(dx, dz):
        return (m, (lax.rem(x + dx, NX) * NZ + lax.rem(z + dz, NZ)) * NC + c, r)

    offsets = sorted(
        ((dx, dz) for dx in range(NX) for dz in range(NZ) if dx or dz),
        key=lambda o: -min(o[0], NX - o[0]) - min(o[1], NZ - o[1]),
    )

    def hid_copy(k):
        at = pl.ds(pl.multiple_of(quarters[k] * Q, Q), Q)
        return pltpu.make_async_copy(hid.at[0, at], xraw.at[k], hid_sem.at[k])

    c_gain = pltpu.make_async_copy(gain, g_buf, ld_sem.at[1])
    c_w = pltpu.make_async_copy(wts, wb, ld_sem.at[2])
    c_gain.start()
    for k in range(4):
        hid_copy(k).start()

    def head_copy(j):
        cols = pl.ds(pl.multiple_of(j * CW, CW), CW)
        return pltpu.make_async_copy(head.at[0, :, cols], hb.at[j], hd_sem.at[j])

    head_copy(0).start()
    lists = [
        pltpu.make_async_copy(src, dst, ld_sem.at[3 + i])
        for i, (src, dst) in enumerate(
            ((psrc_in, psrc), (ptgt_in, ptgt), (pcnt_in, pcnt), (ntok_in, ntok))
        )
    ]
    for cp in lists:
        cp.start()

    barrier = pltpu.get_barrier_semaphore()
    greet = peers + [(m, v_up, r), (m, v_down, r)] + [far(*o) for o in offsets]
    for d in greet:
        pl.semaphore_signal(barrier, inc=1, device_id=d, device_id_type=MESH)

    rows_i = lax.broadcasted_iota(jnp.int32, (Q, Q), 0)
    cols_i = lax.broadcasted_iota(jnp.int32, (Q, Q), 1)
    eye = rows_i == cols_i

    def to_row(col):
        return jnp.sum(jnp.where(eye, col, 0.0), axis=0, keepdims=True)

    def to_col(row):
        return jnp.sum(jnp.where(eye, row, 0.0), axis=1, keepdims=True)

    for edge, at in ((v == 0, 0), (v == 63, 2 * NCH)):

        @pl.when(edge)
        def _(at=at):
            pq[at : at + NCH] = jnp.zeros((NCH, Q, CW), jnp.bfloat16)
            pm[at : at + NCH] = jnp.zeros((NCH, 1, Q), jnp.float32)

    c_gain.wait()
    for k in range(4):
        hid_copy(k).wait()
    for j in range(1, NCH):
        head_copy(j).start()
    c_w.start()
    g = g_buf[...].astype(jnp.float32)

    def prepare(k):
        a = xraw[k].astype(jnp.float32) * g
        hi = a.astype(jnp.bfloat16)
        x2[k * 2 * Q : k * 2 * Q + Q, :] = hi
        x2[k * 2 * Q + Q : (k + 1) * 2 * Q, :] = (a - hi.astype(jnp.float32)).astype(jnp.bfloat16)

    def squares(k):
        a = xraw[k].astype(jnp.float32)
        sq = to_row(jnp.sum(a * a, axis=1, keepdims=True))
        if k < 3:
            sndm[1, k, 1:2, :] = sq
        else:
            own_sq[...] = sq

    def y_copy(j, k):
        return pltpu.make_async_remote_copy(
            src_ref=snd.at[j, k], dst_ref=rcv.at[j, k], send_sem=ys, recv_sem=yr.at[j],
            device_id=peers[k], device_id_type=MESH,
        )

    def ym_copy(j, k):
        return pltpu.make_async_remote_copy(
            src_ref=sndm.at[j, k], dst_ref=rcvm.at[j, k], send_sem=yms, recv_sem=ymr.at[j],
            device_id=peers[k], device_id_type=MESH,
        )

    def multiply(j, k):
        p2 = jnp.dot(x2[k * 2 * Q : (k + 1) * 2 * Q, :], hb[j], preferred_element_type=jnp.float32)
        p = p2[:Q] + p2[Q:]
        if k == 3:
            own[j] = p
        else:
            part[j % 2, k] = p

    def pack(j):
        for k in range(3):
            p = part[j % 2, k]
            top = jnp.maximum(jnp.max(jnp.abs(p), axis=1, keepdims=True), 1e-30)
            snd[j, k] = jnp.round(p * (32767.0 / top)).astype(jnp.int32).astype(jnp.int16)
            sndm[j, k, 0:1, :] = to_row(top * (1.0 / 32767.0))

    def send(j):
        for k in (2, 0, 1):
            y_copy(j, k).start()
        for k in range(3):
            ym_copy(j, k).start()

    def wait_all(ref, sem):
        pltpu.make_async_copy(ref, ref, sem).wait()

    head_copy(0).wait()
    for k in range(3):
        prepare(k)
        multiply(0, k)
    pack(0)
    pl.semaphore_wait(barrier, len(greet))
    send(0)
    prepare(3)
    head_copy(1).wait()
    for k in range(3):
        multiply(1, k)
    for k in range(4):
        squares(k)
    pack(1)
    send(1)
    multiply(0, 3)
    multiply(1, 3)
    for j in range(2, NCH + 1):
        if j < NCH:
            head_copy(j).wait()
            for k in range(4):
                multiply(j, k)
        if j > 2:
            pack(j - 1)
            send(j - 1)

    has = (v < 63, v > 0)

    def halo(j, d):
        target, slot = (((m, v_up, r), j), ((m, v_down, r), 2 * NCH + j))[d]
        return [
            pltpu.make_async_remote_copy(
                src_ref=buf.at[NCH + j], dst_ref=buf.at[slot], send_sem=send.at[d], recv_sem=recv.at[d],
                device_id=target, device_id_type=MESH,
            )
            for buf, send, recv in ((pq, hs, hr), (pm, hms, hmr))
        ]

    def halo_start(j):
        for d in range(2):

            @pl.when(has[d])
            def _(d=d):
                for cp in halo(j, d):
                    cp.start()

    for cp in lists:
        cp.wait()
    token = to_col(ntok[...].reshape(1, Q).astype(jnp.float32))
    lane = lax.broadcasted_iota(jnp.int32, (Q, BLOCK), 1).astype(jnp.float32)

    def at_token(start, values):
        base = (v * (NB * BLOCK) + start).astype(jnp.float32)
        hit = lane[:, : values.shape[1]] == token - base
        return jnp.sum(jnp.where(hit, values, 0.0), axis=1, keepdims=True)

    scale_own = scale_other = None
    for j in range(NCH):
        wait_all(rcv.at[j], yr.at[j])
        if j != 1:
            wait_all(rcvm.at[j], ymr.at[j])
        if j == 0:
            wait_all(rcvm.at[1], ymr.at[1])
            sq = [rcvm[1, k, 1:2, :] for k in range(3)]
            scale_own = lax.rsqrt((own_sq[...] + sq[2]) * (1.0 / 4096.0) + 1e-05)
            scale_other = lax.rsqrt((sq[0] + sq[1]) * (1.0 / 4096.0) + 1e-05)
        near, cross, far_term = (
            rcv[j, k].astype(jnp.float32)
            * to_col(rcvm[j, k, 0:1, :] * (scale_own if k == 2 else scale_other))
            for k in range(3)
        )
        lg[m] = own[j] * to_col(scale_own) + far_term
        lg[1 - m] = near + cross
        logits = lg[1]
        top = jnp.max(logits, axis=1, keepdims=True)
        e = jnp.exp(logits - top)
        pq[NCH + j] = e.astype(jnp.bfloat16)
        pm[NCH + j] = to_row(top)
        halo_start(j)
        q_sums[j] = to_row(jnp.sum(e, axis=1, keepdims=True))
        logits = lg[0]
        top = jnp.max(logits, axis=1, keepdims=True)
        e = jnp.exp(logits - top)
        el[j] = e
        l_tops[j] = to_row(top)
        l_lse[j] = to_row(top + jnp.log(jnp.sum(e, axis=1, keepdims=True)))
        l_tok[j] = to_row(at_token(j * CW, logits))

    def add(a):
        return jnp.sum(a, axis=0, keepdims=True)

    def log_add(rows):
        top = jnp.max(rows, axis=0, keepdims=True)
        return top + jnp.log(add(jnp.exp(rows - top)))

    def merge_l(lse, tok):
        return log_add(lse), add(tok)

    def core_copy(src, dst, i):
        return pltpu.make_async_remote_copy(
            src_ref=src, dst_ref=dst, send_sem=cs.at[i], recv_sem=cs.at[i + 1],
            device_id=core_peer, device_id_type=MESH,
        )

    def spread(ref, send, recv):
        return [
            pltpu.make_async_remote_copy(
                src_ref=ref.at[0], dst_ref=ref.at[dx * NZ + dz], send_sem=send,
                recv_sem=recv, device_id=far(dx, dz), device_id_type=MESH,
            )
            for dx, dz in offsets
        ]

    def both(a, b, i):
        return jnp.concatenate([a[i : i + 1, :], b[i : i + 1, :]], axis=0)

    for i, row in enumerate(merge_l(
        jnp.concatenate([l_lse[j] for j in range(NCH)], axis=0),
        jnp.concatenate([l_tok[j] for j in range(NCH)], axis=0),
    )):
        st_l[i : i + 1, :] = row
    core_l = core_copy(st_l, got_l, 2)
    core_l.start()
    core_l.wait_recv()
    for i, row in enumerate(merge_l(*(both(st_l, got_l, i) for i in range(2)))):
        all_l[0, i : i + 1, :] = row
    spread_l = spread(all_l, lss, lsr)
    for cp in spread_l:
        cp.start()
    c_w.wait()

    for d in range(2):

        @pl.when(has[1 - d])
        def _(d=d):
            slots = pl.ds(2 * NCH * d, NCH)
            wait_all(pq.at[slots], hr.at[d])
            wait_all(pm.at[slots], hmr.at[d])


    live, target, tops, prods = [], [], [], []
    for s in range(4):
        at = 2 * jnp.clip(psrc[s] - (v * NB - NB), 0, 3 * NB - 1)
        for h in range(2):
            live.append((pcnt[0] > s).astype(jnp.float32))
            target.append(ptgt[s] - v * NB)
            tops.append(pm[at + h])
            prods.append(jnp.dot(
                pq[at + h], wb[s, h * CW : (h + 1) * CW, :], preferred_element_type=jnp.float32
            ))
    shift = functools.reduce(
        jnp.maximum, [jnp.where(a > 0.5, t, -jnp.inf) for a, t in zip(live, tops)]
    )
    factors = [
        to_col(jnp.where(a > 0.5, jnp.exp(jnp.minimum(t - shift, 0.0)), 0.0))
        for a, t in zip(live, tops)
    ]
    mass = jnp.zeros((Q, 1), jnp.float32)
    tok_m = jnp.zeros((Q, 1), jnp.float32)
    for t in range(NB):
        total = sum(
            prods[s] * (factors[s] * (target[s] == t).astype(jnp.float32)) for s in range(8)
        )
        mp_buf[t] = total
        mass = mass + jnp.sum(total, axis=1, keepdims=True)
        tok_m = tok_m + at_token(t * BLOCK, total)

    lse_q = log_add(jnp.concatenate(
        [pm[NCH + j] + jnp.log(q_sums[j]) for j in range(NCH)], axis=0
    ))
    tok_row = to_row(tok_m)
    tok_log = jnp.where(tok_row > 0.0, shift + jnp.log(jnp.maximum(tok_row, 1e-37)), -1e30)
    for i, row in enumerate((lse_q, shift + jnp.log(to_row(mass)), tok_log)):
        st_q[i : i + 1, :] = row
    core_q = core_copy(st_q, got_q, 0)
    core_q.start()
    core_q.wait_recv()
    for i in range(2):
        all_q[0, i : i + 1, :] = log_add(both(st_q, got_q, i))
    spread_q = spread(all_q, qss, qsr)
    for cp in spread_q:
        cp.start()
    all_t[0] = log_add(both(st_q, got_q, 2))
    spread_t = spread(all_t, tss, tsr)
    for cp in spread_t:
        cp.start()

    wait_all(snd, ys)
    wait_all(sndm, yms)
    for d in range(2):

        @pl.when(has[d])
        def _(d=d):
            wait_all(pq.at[pl.ds(NCH, NCH)], hs.at[d])
            wait_all(pm.at[pl.ds(NCH, NCH)], hms.at[d])

    core_q.wait_send()
    core_l.wait_send()
    others = pl.ds(1, NX * NZ - 1)
    wait_all(all_q.at[others], qss)
    wait_all(all_l.at[others], lss)
    wait_all(all_t.at[others], tss)
    wait_all(all_l.at[others], lsr)
    lse_l, t_l = merge_l(*(all_l[:, i, :] for i in range(2)))
    for j in range(NCH):
        l_fac[j] = jnp.exp(l_tops[j] - lse_l)
    wait_all(all_q.at[others], qsr)
    total_q, mass_q = (log_add(all_q[:, i, :]) for i in range(2))
    log_norm = jnp.log(1.0 + jnp.exp(mass_q - total_q))
    norm_out[...] = log_norm
    m_fac[...] = jnp.exp(shift - total_q)
    wait_all(all_t.at[others], tsr)
    nll[...] = log_norm - jnp.log(
        jnp.maximum(jnp.exp(t_l - lse_l), FLOOR) + jnp.exp(log_add(all_t[:, 0, :]) - total_q)
    )


def finish(el, mp_buf, l_fac, m_fac, norm_out, nll_in, out, nll, buf, sem):
    rows_i = lax.broadcasted_iota(jnp.int32, (Q, Q), 0)
    cols_i = lax.broadcasted_iota(jnp.int32, (Q, Q), 1)

    def to_col(row):
        return jnp.sum(jnp.where(rows_i == cols_i, row, 0.0), axis=1, keepdims=True)

    copies = [pltpu.make_async_copy(nll_in, nll, sem.at[NCH])]
    copies[0].start()
    norm_col, m_col = to_col(norm_out[...]), to_col(m_fac[...])
    for j in range(NCH):
        at = slice((j % 2) * CW, (j % 2 + 1) * CW)
        mapped = mp_buf[j // 2, :, at]
        buf[:, j * CW : (j + 1) * CW] = (
            jnp.log(jnp.maximum(el[j] * to_col(l_fac[j]), FLOOR) + mapped * m_col) - norm_col
        )
        cols = pl.ds(j * CW, CW)
        copies.append(pltpu.make_async_copy(buf.at[:, cols], out.at[:, cols], sem.at[j]))
        copies[-1].start()
    for cp in copies:
        cp.wait()


def on_device(
    hidden, norm_gain, head_weights, pair_source, pair_target, pair_count, pair_weight, next_token
):
    hbm = pl.BlockSpec(memory_space=pltpu.HBM)
    vmem = pl.BlockSpec(memory_space=pltpu.VMEM)
    dma = pltpu.SemaphoreType.DMA
    f32, bf16 = jnp.float32, jnp.bfloat16
    parts = pl.pallas_call(
        kernel,
        out_shape=(
            pltpu.VMEM((NCH, Q, CW), f32),
            pltpu.VMEM((NB, Q, BLOCK), f32),
            pltpu.VMEM((NCH, 1, Q), f32),
            pltpu.VMEM((1, Q), f32),
            pltpu.VMEM((1, Q), f32),
            pltpu.VMEM((1, Q), f32),
        ),
        in_specs=[pl.BlockSpec(memory_space=pl.ANY)] * 8,
        out_specs=(vmem,) * 6,
        scratch_shapes=[
            pltpu.SMEM((4,), jnp.int32),
            pltpu.SMEM((4,), jnp.int32),
            pltpu.SMEM((1,), jnp.int32),
            pltpu.VMEM((Q,), jnp.int32),
            pltpu.VMEM((4, Q, FEAT), bf16),
            pltpu.VMEM((8 * Q, FEAT), bf16),
            pltpu.VMEM((1, FEAT), bf16),
            pltpu.VMEM((NCH, FEAT, CW), bf16),
            pltpu.VMEM((4, BLOCK, BLOCK), bf16),
            pltpu.VMEM((NCH, 3, Q, CW), jnp.int16),
            pltpu.VMEM((NCH, 3, 2, Q), f32),
            pltpu.VMEM((2, 3, Q, CW), f32),
            pltpu.VMEM((NCH, 3, Q, CW), jnp.int16),
            pltpu.VMEM((NCH, 3, 2, Q), f32),
            pltpu.VMEM((NCH, Q, CW), f32),
            pltpu.VMEM((1, Q), f32),
            pltpu.VMEM((2, Q, CW), f32),
            pltpu.VMEM((3 * NCH, Q, CW), bf16),
            pltpu.VMEM((3 * NCH, 1, Q), f32),
            pltpu.VMEM((NCH, 1, Q), f32),
            pltpu.VMEM((NCH, 1, Q), f32),
            pltpu.VMEM((NCH, 1, Q), f32),
            pltpu.VMEM((NCH, 1, Q), f32),
            pltpu.VMEM((4, Q), f32),
            pltpu.VMEM((4, Q), f32),
            pltpu.VMEM((NX * NZ, 2, Q), f32),
            pltpu.VMEM((NX * NZ, 1, Q), f32),
            pltpu.VMEM((2, Q), f32),
            pltpu.VMEM((2, Q), f32),
            pltpu.VMEM((NX * NZ, 2, Q), f32),
            dma((7,)),
            dma((4,)),
            dma((NCH,)),
            dma(()),
            dma((NCH,)),
            dma(()),
            dma((NCH,)),
            dma((2,)),
            dma((2,)),
            dma((2,)),
            dma((2,)),
            dma((4,)),
            dma(()),
            dma(()),
            dma(()),
            dma(()),
            dma(()),
            dma(()),
        ],
        compiler_params=pltpu.CompilerParams(
            collective_id=0, has_side_effects=True, vmem_limit_bytes=40 * 2**20
        ),
        cost_estimate=pl.CostEstimate(
            flops=4 * 4 * Q * FEAT * NB * BLOCK, bytes_accessed=12 * 2**20, transcendentals=10**6
        ),
        name="ensemble",
    )(
        *(a if a.shape == (1,) else pltpu.with_memory_space_constraint(a, pltpu.HBM) for a in (
            hidden, norm_gain, head_weights, pair_source, pair_target, pair_count, pair_weight,
            next_token,
        ))
    )
    ensemble, nll = pl.pallas_call(
        finish,
        out_shape=(
            jax.ShapeDtypeStruct((Q, NB * BLOCK), f32),
            jax.ShapeDtypeStruct((1, Q), f32),
        ),
        in_specs=[vmem] * 6,
        out_specs=(pl.BlockSpec(memory_space=pl.ANY),) * 2,
        scratch_shapes=[pltpu.VMEM((Q, NB * BLOCK), f32), dma((NCH + 1,))],
        compiler_params=pltpu.CompilerParams(vmem_limit_bytes=32 * 2**20),
        name="finish",
    )(*parts)
    return ensemble, nll.reshape(Q)


def solution(mesh):
    in_specs = (
        P("mp", None, "rows"),
        P("mp", "rows"),
        P("mp", "rows", "vocab"),
        P("vocab"),
        P("vocab"),
        P("vocab"),
        P("vocab", None, None),
        P(("mp", "rows")),
    )
    out_specs = (P(("mp", "rows"), "vocab"), P(("mp", "rows")))
    return jax.shard_map(
        on_device, mesh=mesh, in_specs=in_specs, out_specs=out_specs, check_vma=False
    )
```

```python
import functools

import jax
import jax.numpy as jnp
from jax import lax
from jax.experimental import pallas as pl
from jax.experimental.pallas import tpu as pltpu
from jax.sharding import PartitionSpec as P

MESH = pl.DeviceIdType.MESH
NX, NZ, NC = 4, 8, 2
Q = 128
CW = 256
BLOCK = 512
NCH = 6
NB = 3
FEAT = 2048
FLOOR = 1.9287498479639178e-22


def kernel(
    hid, gain, head, psrc_in, ptgt_in, pcnt_in, wts, ntok_in,
    el, mp_buf, l_fac, m_fac, norm_out, nll,
    psrc, ptgt, pcnt, ntok, xraw, x2, g_buf, hb, wb, snd, sndm, part, rcv, rcvm, own, own_sq, lg, pq, pm, q_sums,
    l_tops, l_lse, l_tok, st_q, got_q, all_q, all_t, st_l, got_l, all_l,
    ld_sem, hid_sem, hd_sem, ys, yr, yms, ymr, hs, hr, hms, hmr, cs, qss, qsr, lss, lsr, tss, tsr,
):
    m = lax.axis_index("mp")
    v = lax.axis_index("vocab")
    r = lax.axis_index("rows")
    x, z, c = v // (NZ * NC), lax.rem(v // NC, NZ), lax.rem(v, NC)
    v_up, v_down = lax.rem(v + 1, 64), lax.rem(v + 63, 64)

    peers = [(1 - m, v, r), (1 - m, v, 1 - r), (m, v, 1 - r)]
    quarters = [(1 - m) * 2 + r, (1 - m) * 2 + 1 - r, m * 2 + 1 - r, m * 2 + r]
    core_peer = (m, (x * NZ + z) * NC + 1 - c, r)

    def far(dx, dz):
        return (m, (lax.rem(x + dx, NX) * NZ + lax.rem(z + dz, NZ)) * NC + c, r)

    offsets = sorted(
        ((dx, dz) for dx in range(NX) for dz in range(NZ) if dx or dz),
        key=lambda o: -min(o[0], NX - o[0]) - min(o[1], NZ - o[1]),
    )

    def hid_copy(k):
        at = pl.ds(pl.multiple_of(quarters[k] * Q, Q), Q)
        return pltpu.make_async_copy(hid.at[0, at], xraw.at[k], hid_sem.at[k])

    c_gain = pltpu.make_async_copy(gain, g_buf, ld_sem.at[1])
    c_w = pltpu.make_async_copy(wts, wb, ld_sem.at[2])
    c_gain.start()
    for k in range(4):
        hid_copy(k).start()

    def head_copy(j):
        cols = pl.ds(pl.multiple_of(j * CW, CW), CW)
        return pltpu.make_async_copy(head.at[0, :, cols], hb.at[j], hd_sem.at[j])

    head_copy(0).start()
    lists = [
        pltpu.make_async_copy(src, dst, ld_sem.at[3 + i])
        for i, (src, dst) in enumerate(
            ((psrc_in, psrc), (ptgt_in, ptgt), (pcnt_in, pcnt), (ntok_in, ntok))
        )
    ]
    for cp in lists:
        cp.start()

    barrier = pltpu.get_barrier_semaphore()
    greet = peers + [(m, v_up, r), (m, v_down, r)] + [far(*o) for o in offsets]
    for d in greet:
        pl.semaphore_signal(barrier, inc=1, device_id=d, device_id_type=MESH)

    rows_i = lax.broadcasted_iota(jnp.int32, (Q, Q), 0)
    cols_i = lax.broadcasted_iota(jnp.int32, (Q, Q), 1)
    eye = rows_i == cols_i

    def to_row(col):
        return jnp.sum(jnp.where(eye, col, 0.0), axis=0, keepdims=True)

    def to_col(row):
        return jnp.sum(jnp.where(eye, row, 0.0), axis=1, keepdims=True)

    for edge, at in ((v == 0, 0), (v == 63, 2 * NCH)):

        @pl.when(edge)
        def _(at=at):
            pq[at : at + NCH] = jnp.zeros((NCH, Q, CW), jnp.bfloat16)
            pm[at : at + NCH] = jnp.zeros((NCH, 1, Q), jnp.float32)

    c_gain.wait()
    for k in range(4):
        hid_copy(k).wait()
    for j in range(1, NCH):
        head_copy(j).start()
    c_w.start()
    g = g_buf[...].astype(jnp.float32)

    def prepare(k):
        a = xraw[k].astype(jnp.float32) * g
        hi = a.astype(jnp.bfloat16)
        x2[k * 2 * Q : k * 2 * Q + Q, :] = hi
        x2[k * 2 * Q + Q : (k + 1) * 2 * Q, :] = (a - hi.astype(jnp.float32)).astype(jnp.bfloat16)

    def squares(k):
        a = xraw[k].astype(jnp.float32)
        sq = to_row(jnp.sum(a * a, axis=1, keepdims=True))
        if k < 3:
            sndm[1, k, 1:2, :] = sq
        else:
            own_sq[...] = sq

    def halves(j):
        return ((0, Q),) if j < NCH - 1 else ((0, 48), (48, 48), (96, 32))

    def y_copy(j, k, h):
        rows = pl.ds(*halves(j)[h])
        return pltpu.make_async_remote_copy(
            src_ref=snd.at[j, k, rows], dst_ref=rcv.at[j, k, rows], send_sem=ys, recv_sem=yr.at[j + h],
            device_id=peers[k], device_id_type=MESH,
        )

    def ym_copy(j, k):
        return pltpu.make_async_remote_copy(
            src_ref=sndm.at[j, k], dst_ref=rcvm.at[j, k], send_sem=yms, recv_sem=ymr.at[j],
            device_id=peers[k], device_id_type=MESH,
        )

    def multiply(j, k):
        p2 = jnp.dot(x2[k * 2 * Q : (k + 1) * 2 * Q, :], hb[j], preferred_element_type=jnp.float32)
        p = p2[:Q] + p2[Q:]
        if k == 3:
            own[j] = p
        else:
            part[j % 2, k] = p

    def pack(j):
        for k in range(3):
            p = part[j % 2, k]
            top = jnp.maximum(jnp.max(jnp.abs(p), axis=1, keepdims=True), 1e-30)
            snd[j, k] = jnp.round(p * (32767.0 / top)).astype(jnp.int32).astype(jnp.int16)
            sndm[j, k, 0:1, :] = to_row(top * (1.0 / 32767.0))

    def send(j):
        for k in (2, 0, 1):
            y_copy(j, k, 0).start()
        for k in range(3):
            ym_copy(j, k).start()
        for h in range(1, len(halves(j))):
            for k in (2, 0, 1):
                y_copy(j, k, h).start()

    def wait_all(ref, sem):
        pltpu.make_async_copy(ref, ref, sem).wait()

    head_copy(0).wait()
    for k in range(3):
        prepare(k)
        multiply(0, k)
    pack(0)
    pl.semaphore_wait(barrier, len(greet))
    send(0)
    prepare(3)
    head_copy(1).wait()
    for k in range(3):
        multiply(1, k)
    for k in range(4):
        squares(k)
    pack(1)
    send(1)
    multiply(0, 3)
    multiply(1, 3)
    for j in range(2, NCH + 1):
        if j < NCH:
            head_copy(j).wait()
            for k in range(4):
                multiply(j, k)
        if j > 2:
            pack(j - 1)
            send(j - 1)

    has = (v < 63, v > 0)

    def halo(buf, j, d, rows, send, recv):
        target, slot = (((m, v_up, r), j), ((m, v_down, r), 2 * NCH + j))[d]
        return pltpu.make_async_remote_copy(
            src_ref=buf.at[NCH + j, rows], dst_ref=buf.at[slot, rows], send_sem=send.at[d], recv_sem=recv.at[d],
            device_id=target, device_id_type=MESH,
        )

    def halo_start(j, h):
        for d in range(2):

            @pl.when(has[d])
            def _(d=d):
                halo(pq, j, d, pl.ds(*halves(j)[h]), hs, hr).start()
                if h == len(halves(j)) - 1:
                    halo(pm, j, d, pl.ds(0, 1), hms, hmr).start()

    for cp in lists:
        cp.wait()
    token = to_col(ntok[...].reshape(1, Q).astype(jnp.float32))
    lane = lax.broadcasted_iota(jnp.int32, (Q, BLOCK), 1).astype(jnp.float32)

    def at_token(start, values):
        base = (v * (NB * BLOCK) + start).astype(jnp.float32)
        hit = lane[:, : values.shape[1]] == token - base
        return jnp.sum(jnp.where(hit, values, 0.0), axis=1, keepdims=True)

    scale_own = scale_other = None
    for j in range(NCH):
        if j != 1:
            wait_all(rcvm.at[j], ymr.at[j])
        if j == 0:
            wait_all(rcvm.at[1], ymr.at[1])
            sq = [rcvm[1, k, 1:2, :] for k in range(3)]
            scale_own = lax.rsqrt((own_sq[...] + sq[2]) * (1.0 / 4096.0) + 1e-05)
            scale_other = lax.rsqrt((sq[0] + sq[1]) * (1.0 / 4096.0) + 1e-05)
        own_col = to_col(scale_own)
        cols = [
            to_col(rcvm[j, k, 0:1, :] * (scale_own if k == 2 else scale_other)) for k in range(3)
        ]
        q_tops, q_parts = [], []
        for h, (first, count) in enumerate(halves(j)):
            at = slice(first, first + count)
            wait_all(rcv.at[j, :, pl.ds(first, count)], yr.at[j + h])
            near, cross, far_term = (
                rcv[j, k, at].astype(jnp.float32) * cols[k][at] for k in range(3)
            )
            lg[m, at] = own[j, at] * own_col[at] + far_term
            lg[1 - m, at] = near + cross
            logits = lg[1, at]
            top = jnp.max(logits, axis=1, keepdims=True)
            e = jnp.exp(logits - top)
            pq[NCH + j, at] = e.astype(jnp.bfloat16)
            q_tops.append(top)
            q_parts.append(jnp.sum(e, axis=1, keepdims=True))
            if h == len(halves(j)) - 1:
                pm[NCH + j] = to_row(jnp.concatenate(q_tops, axis=0))
            halo_start(j, h)
        q_sums[j] = to_row(jnp.concatenate(q_parts, axis=0))
        logits = lg[0]
        top = jnp.max(logits, axis=1, keepdims=True)
        e = jnp.exp(logits - top)
        el[j] = e
        l_tops[j] = to_row(top)
        l_lse[j] = to_row(top + jnp.log(jnp.sum(e, axis=1, keepdims=True)))
        l_tok[j] = to_row(at_token(j * CW, logits))

    def add(a):
        return jnp.sum(a, axis=0, keepdims=True)

    def log_add(rows):
        top = jnp.max(rows, axis=0, keepdims=True)
        return top + jnp.log(add(jnp.exp(rows - top)))

    def merge_l(lse, tok):
        return log_add(lse), add(tok)

    def core_copy(src, dst, i):
        return pltpu.make_async_remote_copy(
            src_ref=src, dst_ref=dst, send_sem=cs.at[i], recv_sem=cs.at[i + 1],
            device_id=core_peer, device_id_type=MESH,
        )

    def spread(ref, send, recv):
        return [
            pltpu.make_async_remote_copy(
                src_ref=ref.at[0], dst_ref=ref.at[dx * NZ + dz], send_sem=send,
                recv_sem=recv, device_id=far(dx, dz), device_id_type=MESH,
            )
            for dx, dz in offsets
        ]

    def both(a, b, i):
        return jnp.concatenate([a[i : i + 1, :], b[i : i + 1, :]], axis=0)

    for i, row in enumerate(merge_l(
        jnp.concatenate([l_lse[j] for j in range(NCH)], axis=0),
        jnp.concatenate([l_tok[j] for j in range(NCH)], axis=0),
    )):
        st_l[i : i + 1, :] = row
    core_l = core_copy(st_l, got_l, 2)
    core_l.start()
    core_l.wait_recv()
    for i, row in enumerate(merge_l(*(both(st_l, got_l, i) for i in range(2)))):
        all_l[0, i : i + 1, :] = row
    spread_l = spread(all_l, lss, lsr)
    for cp in spread_l:
        cp.start()
    c_w.wait()

    for d in range(2):

        @pl.when(has[1 - d])
        def _(d=d):
            slots = pl.ds(2 * NCH * d, NCH)
            wait_all(pq.at[slots], hr.at[d])
            wait_all(pm.at[slots], hmr.at[d])


    live, target, tops, prods = [], [], [], []
    for s in range(4):
        at = 2 * jnp.clip(psrc[s] - (v * NB - NB), 0, 3 * NB - 1)
        for h in range(2):
            live.append((pcnt[0] > s).astype(jnp.float32))
            target.append(ptgt[s] - v * NB)
            tops.append(pm[at + h])
            prods.append(jnp.dot(
                pq[at + h], wb[s, h * CW : (h + 1) * CW, :], preferred_element_type=jnp.float32
            ))
    shift = functools.reduce(
        jnp.maximum, [jnp.where(a > 0.5, t, -jnp.inf) for a, t in zip(live, tops)]
    )
    factors = [
        to_col(jnp.where(a > 0.5, jnp.exp(jnp.minimum(t - shift, 0.0)), 0.0))
        for a, t in zip(live, tops)
    ]
    mass = jnp.zeros((Q, 1), jnp.float32)
    tok_m = jnp.zeros((Q, 1), jnp.float32)
    for t in range(NB):
        total = sum(
            prods[s] * (factors[s] * (target[s] == t).astype(jnp.float32)) for s in range(8)
        )
        mp_buf[t] = total
        mass = mass + jnp.sum(total, axis=1, keepdims=True)
        tok_m = tok_m + at_token(t * BLOCK, total)

    lse_q = log_add(jnp.concatenate(
        [pm[NCH + j] + jnp.log(q_sums[j]) for j in range(NCH)], axis=0
    ))
    tok_row = to_row(tok_m)
    tok_log = jnp.where(tok_row > 0.0, shift + jnp.log(jnp.maximum(tok_row, 1e-37)), -1e30)
    for i, row in enumerate((lse_q, shift + jnp.log(to_row(mass)), tok_log)):
        st_q[i : i + 1, :] = row
    core_q = core_copy(st_q, got_q, 0)
    core_q.start()
    core_q.wait_recv()
    for i in range(2):
        all_q[0, i : i + 1, :] = log_add(both(st_q, got_q, i))
    spread_q = spread(all_q, qss, qsr)
    for cp in spread_q:
        cp.start()
    all_t[0] = log_add(both(st_q, got_q, 2))
    spread_t = spread(all_t, tss, tsr)
    for cp in spread_t:
        cp.start()

    wait_all(snd, ys)
    wait_all(sndm, yms)
    for d in range(2):

        @pl.when(has[d])
        def _(d=d):
            wait_all(pq.at[pl.ds(NCH, NCH)], hs.at[d])
            wait_all(pm.at[pl.ds(NCH, NCH)], hms.at[d])

    core_q.wait_send()
    core_l.wait_send()
    others = pl.ds(1, NX * NZ - 1)
    wait_all(all_q.at[others], qss)
    wait_all(all_l.at[others], lss)
    wait_all(all_t.at[others], tss)
    wait_all(all_l.at[others], lsr)
    lse_l, t_l = merge_l(*(all_l[:, i, :] for i in range(2)))
    for j in range(NCH):
        l_fac[j] = jnp.exp(l_tops[j] - lse_l)
    wait_all(all_q.at[others], qsr)
    total_q, mass_q = (log_add(all_q[:, i, :]) for i in range(2))
    log_norm = jnp.log(1.0 + jnp.exp(mass_q - total_q))
    norm_out[...] = log_norm
    m_fac[...] = jnp.exp(shift - total_q)
    wait_all(all_t.at[others], tsr)
    nll[...] = log_norm - jnp.log(
        jnp.maximum(jnp.exp(t_l - lse_l), FLOOR) + jnp.exp(log_add(all_t[:, 0, :]) - total_q)
    )


def finish(el, mp_buf, l_fac, m_fac, norm_out, nll_in, out, nll, buf, sem):
    rows_i = lax.broadcasted_iota(jnp.int32, (Q, Q), 0)
    cols_i = lax.broadcasted_iota(jnp.int32, (Q, Q), 1)

    def to_col(row):
        return jnp.sum(jnp.where(rows_i == cols_i, row, 0.0), axis=1, keepdims=True)

    copies = [pltpu.make_async_copy(nll_in, nll, sem.at[NCH])]
    copies[0].start()
    norm_col, m_col = to_col(norm_out[...]), to_col(m_fac[...])
    for j in range(NCH):
        at = slice((j % 2) * CW, (j % 2 + 1) * CW)
        mapped = mp_buf[j // 2, :, at]
        buf[:, j * CW : (j + 1) * CW] = (
            jnp.log(jnp.maximum(el[j] * to_col(l_fac[j]), FLOOR) + mapped * m_col) - norm_col
        )
        cols = pl.ds(j * CW, CW)
        copies.append(pltpu.make_async_copy(buf.at[:, cols], out.at[:, cols], sem.at[j]))
        copies[-1].start()
    for cp in copies:
        cp.wait()


def on_device(
    hidden, norm_gain, head_weights, pair_source, pair_target, pair_count, pair_weight, next_token
):
    hbm = pl.BlockSpec(memory_space=pltpu.HBM)
    vmem = pl.BlockSpec(memory_space=pltpu.VMEM)
    dma = pltpu.SemaphoreType.DMA
    f32, bf16 = jnp.float32, jnp.bfloat16
    parts = pl.pallas_call(
        kernel,
        out_shape=(
            pltpu.VMEM((NCH, Q, CW), f32),
            pltpu.VMEM((NB, Q, BLOCK), f32),
            pltpu.VMEM((NCH, 1, Q), f32),
            pltpu.VMEM((1, Q), f32),
            pltpu.VMEM((1, Q), f32),
            pltpu.VMEM((1, Q), f32),
        ),
        in_specs=[pl.BlockSpec(memory_space=pl.ANY)] * 8,
        out_specs=(vmem,) * 6,
        scratch_shapes=[
            pltpu.SMEM((4,), jnp.int32),
            pltpu.SMEM((4,), jnp.int32),
            pltpu.SMEM((1,), jnp.int32),
            pltpu.VMEM((Q,), jnp.int32),
            pltpu.VMEM((4, Q, FEAT), bf16),
            pltpu.VMEM((8 * Q, FEAT), bf16),
            pltpu.VMEM((1, FEAT), bf16),
            pltpu.VMEM((NCH, FEAT, CW), bf16),
            pltpu.VMEM((4, BLOCK, BLOCK), bf16),
            pltpu.VMEM((NCH, 3, Q, CW), jnp.int16),
            pltpu.VMEM((NCH, 3, 2, Q), f32),
            pltpu.VMEM((2, 3, Q, CW), f32),
            pltpu.VMEM((NCH, 3, Q, CW), jnp.int16),
            pltpu.VMEM((NCH, 3, 2, Q), f32),
            pltpu.VMEM((NCH, Q, CW), f32),
            pltpu.VMEM((1, Q), f32),
            pltpu.VMEM((2, Q, CW), f32),
            pltpu.VMEM((3 * NCH, Q, CW), bf16),
            pltpu.VMEM((3 * NCH, 1, Q), f32),
            pltpu.VMEM((NCH, 1, Q), f32),
            pltpu.VMEM((NCH, 1, Q), f32),
            pltpu.VMEM((NCH, 1, Q), f32),
            pltpu.VMEM((NCH, 1, Q), f32),
            pltpu.VMEM((3, Q), f32),
            pltpu.VMEM((3, Q), f32),
            pltpu.VMEM((NX * NZ, 2, Q), f32),
            pltpu.VMEM((NX * NZ, 1, Q), f32),
            pltpu.VMEM((2, Q), f32),
            pltpu.VMEM((2, Q), f32),
            pltpu.VMEM((NX * NZ, 2, Q), f32),
            dma((7,)),
            dma((4,)),
            dma((NCH,)),
            dma(()),
            dma((NCH + 2,)),
            dma(()),
            dma((NCH,)),
            dma((2,)),
            dma((2,)),
            dma((2,)),
            dma((2,)),
            dma((4,)),
            dma(()),
            dma(()),
            dma(()),
            dma(()),
            dma(()),
            dma(()),
        ],
        compiler_params=pltpu.CompilerParams(
            collective_id=0, has_side_effects=True, vmem_limit_bytes=40 * 2**20
        ),
        cost_estimate=pl.CostEstimate(
            flops=4 * 4 * Q * FEAT * NB * BLOCK, bytes_accessed=12 * 2**20, transcendentals=10**6
        ),
        name="ensemble",
    )(
        *(a if a.shape == (1,) else pltpu.with_memory_space_constraint(a, pltpu.HBM) for a in (
            hidden, norm_gain, head_weights, pair_source, pair_target, pair_count, pair_weight,
            next_token,
        ))
    )
    ensemble, nll = pl.pallas_call(
        finish,
        out_shape=(
            jax.ShapeDtypeStruct((Q, NB * BLOCK), f32),
            jax.ShapeDtypeStruct((1, Q), f32),
        ),
        in_specs=[vmem] * 6,
        out_specs=(pl.BlockSpec(memory_space=pl.ANY),) * 2,
        scratch_shapes=[pltpu.VMEM((Q, NB * BLOCK), f32), dma((NCH + 2,))],
        compiler_params=pltpu.CompilerParams(vmem_limit_bytes=32 * 2**20),
        name="finish",
    )(*parts)
    return ensemble, nll.reshape(Q)


def solution(mesh):
    in_specs = (
        P("mp", None, "rows"),
        P("mp", "rows"),
        P("mp", "rows", "vocab"),
        P("vocab"),
        P("vocab"),
        P("vocab"),
        P("vocab", None, None),
        P(("mp", "rows")),
    )
    out_specs = (P(("mp", "rows"), "vocab"), P(("mp", "rows")))
    return jax.shard_map(
        on_device, mesh=mesh, in_specs=in_specs, out_specs=out_specs, check_vma=False
    )
```

```python
import functools

import jax
import jax.numpy as jnp
from jax import lax
from jax.experimental import pallas as pl
from jax.experimental.pallas import tpu as pltpu
from jax.sharding import PartitionSpec as P

MESH = pl.DeviceIdType.MESH
NX, NZ, NC = 4, 8, 2
Q = 128
CW = 256
BLOCK = 512
NCH = 6
NB = 3
FEAT = 2048
FLOOR = 1.9287498479639178e-22


def kernel(
    hid, gain, head, psrc_in, ptgt_in, pcnt_in, wts, ntok_in,
    el, mp_buf, l_fac, m_fac, norm_out, nll,
    psrc, ptgt, pcnt, ntok, xraw, x2, g_buf, hb, wb, snd, sndm, part, rcv, rcvm, own, own_sq, lg, pq, pm, q_sums,
    l_tops, l_lse, l_tok, st_q, got_q, all_q, all_t, st_l, got_l, all_l,
    ld_sem, hid_sem, hd_sem, ys, yr, yms, ymr, hs, hr, hms, hmr, cs, qss, qsr, lss, lsr, tss, tsr,
):
    m = lax.axis_index("mp")
    v = lax.axis_index("vocab")
    r = lax.axis_index("rows")
    x, z, c = v // (NZ * NC), lax.rem(v // NC, NZ), lax.rem(v, NC)
    v_up, v_down = lax.rem(v + 1, 64), lax.rem(v + 63, 64)

    peers = [(1 - m, v, r), (1 - m, v, 1 - r), (m, v, 1 - r)]
    quarters = [(1 - m) * 2 + r, (1 - m) * 2 + 1 - r, m * 2 + 1 - r, m * 2 + r]
    core_peer = (m, (x * NZ + z) * NC + 1 - c, r)

    def far(dx, dz):
        return (m, (lax.rem(x + dx, NX) * NZ + lax.rem(z + dz, NZ)) * NC + c, r)

    offsets = sorted(
        ((dx, dz) for dx in range(NX) for dz in range(NZ) if dx or dz),
        key=lambda o: -min(o[0], NX - o[0]) - min(o[1], NZ - o[1]),
    )

    def hid_copy(k):
        at = pl.ds(pl.multiple_of(quarters[k] * Q, Q), Q)
        return pltpu.make_async_copy(hid.at[0, at], xraw.at[k], hid_sem.at[k])

    c_gain = pltpu.make_async_copy(gain, g_buf, ld_sem.at[1])
    c_w = pltpu.make_async_copy(wts, wb, ld_sem.at[2])
    c_gain.start()
    for k in range(4):
        hid_copy(k).start()

    def head_copy(j):
        cols = pl.ds(pl.multiple_of(j * CW, CW), CW)
        return pltpu.make_async_copy(head.at[0, :, cols], hb.at[j], hd_sem.at[j])

    head_copy(0).start()
    lists = [
        pltpu.make_async_copy(src, dst, ld_sem.at[3 + i])
        for i, (src, dst) in enumerate(
            ((psrc_in, psrc), (ptgt_in, ptgt), (pcnt_in, pcnt), (ntok_in, ntok))
        )
    ]
    for cp in lists:
        cp.start()

    barrier = pltpu.get_barrier_semaphore()
    greet = peers + [(m, v_up, r), (m, v_down, r)] + [far(*o) for o in offsets]
    for d in greet:
        pl.semaphore_signal(barrier, inc=1, device_id=d, device_id_type=MESH)

    rows_i = lax.broadcasted_iota(jnp.int32, (Q, Q), 0)
    cols_i = lax.broadcasted_iota(jnp.int32, (Q, Q), 1)
    eye = rows_i == cols_i

    def to_row(col):
        return jnp.sum(jnp.where(eye, col, 0.0), axis=0, keepdims=True)

    def to_col(row):
        return jnp.sum(jnp.where(eye, row, 0.0), axis=1, keepdims=True)

    for edge, at in ((v == 0, 0), (v == 63, 2 * NCH)):

        @pl.when(edge)
        def _(at=at):
            pq[at : at + NCH] = jnp.zeros((NCH, Q, CW), jnp.bfloat16)
            pm[at : at + NCH] = jnp.zeros((NCH, 1, Q), jnp.float32)

    c_gain.wait()
    for k in range(4):
        hid_copy(k).wait()
    for j in range(1, NCH):
        head_copy(j).start()
    c_w.start()
    g = g_buf[...].astype(jnp.float32)

    def prepare(k):
        a = xraw[k].astype(jnp.float32) * g
        hi = a.astype(jnp.bfloat16)
        x2[k * 2 * Q : k * 2 * Q + Q, :] = hi
        x2[k * 2 * Q + Q : (k + 1) * 2 * Q, :] = (a - hi.astype(jnp.float32)).astype(jnp.bfloat16)

    def squares(k):
        a = xraw[k].astype(jnp.float32)
        sq = to_row(jnp.sum(a * a, axis=1, keepdims=True))
        if k < 3:
            sndm[1, k, 1:2, :] = sq
        else:
            own_sq[...] = sq

    def halves(j):
        return ((0, Q),) if j < NCH - 1 else ((0, 48), (48, 48), (96, 32))

    def y_copy(j, k, h):
        rows = pl.ds(*halves(j)[h])
        return pltpu.make_async_remote_copy(
            src_ref=snd.at[j, k, rows], dst_ref=rcv.at[j, k, rows], send_sem=ys, recv_sem=yr.at[j + h],
            device_id=peers[k], device_id_type=MESH,
        )

    def ym_copy(j, k):
        return pltpu.make_async_remote_copy(
            src_ref=sndm.at[j, k], dst_ref=rcvm.at[j, k], send_sem=yms, recv_sem=ymr.at[j],
            device_id=peers[k], device_id_type=MESH,
        )

    def multiply(j, k):
        p2 = jnp.dot(x2[k * 2 * Q : (k + 1) * 2 * Q, :], hb[j], preferred_element_type=jnp.float32)
        p = p2[:Q] + p2[Q:]
        if k == 3:
            own[j] = p
        else:
            part[j % 2, k] = p

    def pack(j):
        for k in range(3):
            p = part[j % 2, k]
            top = jnp.maximum(jnp.max(jnp.abs(p), axis=1, keepdims=True), 1e-30)
            snd[j, k] = jnp.round(p * (32767.0 / top)).astype(jnp.int32).astype(jnp.int16)
            sndm[j, k, 0:1, :] = to_row(top * (1.0 / 32767.0))

    def send(j):
        for k in (2, 0, 1):
            y_copy(j, k, 0).start()
        for k in range(3):
            ym_copy(j, k).start()
        for h in range(1, len(halves(j))):
            for k in (2, 0, 1):
                y_copy(j, k, h).start()

    def wait_all(ref, sem):
        pltpu.make_async_copy(ref, ref, sem).wait()

    head_copy(0).wait()
    for k in range(3):
        prepare(k)
        multiply(0, k)
    pack(0)
    pl.semaphore_wait(barrier, len(greet))
    send(0)
    prepare(3)
    head_copy(1).wait()
    for k in range(3):
        multiply(1, k)
    for k in range(4):
        squares(k)
    pack(1)
    send(1)
    multiply(0, 3)
    multiply(1, 3)
    for j in range(2, NCH + 1):
        if j < NCH:
            head_copy(j).wait()
            for k in range(4):
                multiply(j, k)
        if j > 2:
            pack(j - 1)
            send(j - 1)

    has = (v < 63, v > 0)

    def halo(buf, j, d, rows, send, recv):
        target, slot = (((m, v_up, r), j), ((m, v_down, r), 2 * NCH + j))[d]
        return pltpu.make_async_remote_copy(
            src_ref=buf.at[NCH + j, rows], dst_ref=buf.at[slot, rows], send_sem=send.at[d], recv_sem=recv.at[d],
            device_id=target, device_id_type=MESH,
        )

    def halo_start(j, h):
        for d in range(2):

            @pl.when(has[d])
            def _(d=d):
                halo(pq, j, d, pl.ds(*halves(j)[h]), hs, hr).start()
                if h == len(halves(j)) - 1:
                    halo(pm, j, d, pl.ds(0, 1), hms, hmr).start()

    for cp in lists:
        cp.wait()
    token = to_col(ntok[...].reshape(1, Q).astype(jnp.float32))
    lane = lax.broadcasted_iota(jnp.int32, (Q, BLOCK), 1).astype(jnp.float32)

    def at_token(start, values):
        base = (v * (NB * BLOCK) + start).astype(jnp.float32)
        hit = lane[:, : values.shape[1]] == token - base
        return jnp.sum(jnp.where(hit, values, 0.0), axis=1, keepdims=True)

    scale_own = scale_other = None
    for j in range(NCH):
        if j != 1:
            wait_all(rcvm.at[j], ymr.at[j])
        if j == 0:
            wait_all(rcvm.at[1], ymr.at[1])
            sq = [rcvm[1, k, 1:2, :] for k in range(3)]
            scale_own = lax.rsqrt((own_sq[...] + sq[2]) * (1.0 / 4096.0) + 1e-05)
            scale_other = lax.rsqrt((sq[0] + sq[1]) * (1.0 / 4096.0) + 1e-05)
        own_col = to_col(scale_own)
        cols = [
            to_col(rcvm[j, k, 0:1, :] * (scale_own if k == 2 else scale_other)) for k in range(3)
        ]
        q_tops, q_parts = [], []
        for h, (first, count) in enumerate(halves(j)):
            at = slice(first, first + count)
            wait_all(rcv.at[j, :, pl.ds(first, count)], yr.at[j + h])
            near, cross, far_term = (
                rcv[j, k, at].astype(jnp.float32) * cols[k][at] for k in range(3)
            )
            lg[m, at] = own[j, at] * own_col[at] + far_term
            lg[1 - m, at] = near + cross
            logits = lg[1, at]
            top = jnp.max(logits, axis=1, keepdims=True)
            e = jnp.exp(logits - top)
            pq[NCH + j, at] = e.astype(jnp.bfloat16)
            q_tops.append(top)
            q_parts.append(jnp.sum(e, axis=1, keepdims=True))
            if h == len(halves(j)) - 1:
                pm[NCH + j] = to_row(jnp.concatenate(q_tops, axis=0))
            halo_start(j, h)
        q_sums[j] = to_row(jnp.concatenate(q_parts, axis=0))
        logits = lg[0]
        top = jnp.max(logits, axis=1, keepdims=True)
        e = jnp.exp(logits - top)
        el[j] = e
        l_tops[j] = to_row(top)
        l_lse[j] = to_row(top + jnp.log(jnp.sum(e, axis=1, keepdims=True)))
        l_tok[j] = to_row(at_token(j * CW, logits))

    def add(a):
        return jnp.sum(a, axis=0, keepdims=True)

    def log_add(rows):
        top = jnp.max(rows, axis=0, keepdims=True)
        return top + jnp.log(add(jnp.exp(rows - top)))

    def merge_l(lse, tok):
        return log_add(lse), add(tok)

    def core_copy(src, dst, i):
        return pltpu.make_async_remote_copy(
            src_ref=src, dst_ref=dst, send_sem=cs.at[i], recv_sem=cs.at[i + 1],
            device_id=core_peer, device_id_type=MESH,
        )

    def spread(ref, send, recv):
        return [
            pltpu.make_async_remote_copy(
                src_ref=ref.at[0], dst_ref=ref.at[dx * NZ + dz], send_sem=send,
                recv_sem=recv, device_id=far(dx, dz), device_id_type=MESH,
            )
            for dx, dz in offsets
        ]

    def both(a, b, i):
        return jnp.concatenate([a[i : i + 1, :], b[i : i + 1, :]], axis=0)

    for i, row in enumerate(merge_l(
        jnp.concatenate([l_lse[j] for j in range(NCH)], axis=0),
        jnp.concatenate([l_tok[j] for j in range(NCH)], axis=0),
    )):
        st_l[i : i + 1, :] = row
    core_l = core_copy(st_l, got_l, 2)
    core_l.start()
    core_l.wait_recv()
    for i, row in enumerate(merge_l(*(both(st_l, got_l, i) for i in range(2)))):
        all_l[0, i : i + 1, :] = row
    spread_l = spread(all_l, lss, lsr)
    for cp in spread_l:
        cp.start()
    c_w.wait()

    for d in range(2):

        @pl.when(has[1 - d])
        def _(d=d):
            slots = pl.ds(2 * NCH * d, NCH)
            wait_all(pq.at[slots], hr.at[d])
            wait_all(pm.at[slots], hmr.at[d])


    live, target, tops, prods = [], [], [], []
    for s in range(4):
        at = 2 * jnp.clip(psrc[s] - (v * NB - NB), 0, 3 * NB - 1)
        for h in range(2):
            live.append((pcnt[0] > s).astype(jnp.float32))
            target.append(ptgt[s] - v * NB)
            tops.append(pm[at + h])
            prods.append(jnp.dot(
                pq[at + h], wb[s, h * CW : (h + 1) * CW, :], preferred_element_type=jnp.float32
            ))
    shift = functools.reduce(
        jnp.maximum, [jnp.where(a > 0.5, t, -jnp.inf) for a, t in zip(live, tops)]
    )
    factors = [
        to_col(jnp.where(a > 0.5, jnp.exp(jnp.minimum(t - shift, 0.0)), 0.0))
        for a, t in zip(live, tops)
    ]
    mass = jnp.zeros((Q, 1), jnp.float32)
    tok_m = jnp.zeros((Q, 1), jnp.float32)
    terms = [
        prods[2 * s] * factors[2 * s] + prods[2 * s + 1] * factors[2 * s + 1] for s in range(4)
    ]
    for t in range(NB):
        total = sum(terms[s] * (target[2 * s] == t).astype(jnp.float32) for s in range(4))
        mp_buf[t] = total
        mass = mass + jnp.sum(total, axis=1, keepdims=True)
        tok_m = tok_m + at_token(t * BLOCK, total)

    lse_q = log_add(jnp.concatenate(
        [pm[NCH + j] + jnp.log(q_sums[j]) for j in range(NCH)], axis=0
    ))
    tok_row = to_row(tok_m)
    tok_log = jnp.where(tok_row > 0.0, shift + jnp.log(jnp.maximum(tok_row, 1e-37)), -1e30)
    for i, row in enumerate((lse_q, shift + jnp.log(to_row(mass)), tok_log)):
        st_q[i : i + 1, :] = row
    core_q = core_copy(st_q, got_q, 0)
    core_q.start()
    core_q.wait_recv()
    for i in range(2):
        all_q[0, i : i + 1, :] = log_add(both(st_q, got_q, i))
    spread_q = spread(all_q, qss, qsr)
    for cp in spread_q:
        cp.start()
    all_t[0] = log_add(both(st_q, got_q, 2))
    spread_t = spread(all_t, tss, tsr)
    for cp in spread_t:
        cp.start()

    wait_all(snd, ys)
    wait_all(sndm, yms)
    for d in range(2):

        @pl.when(has[d])
        def _(d=d):
            wait_all(pq.at[pl.ds(NCH, NCH)], hs.at[d])
            wait_all(pm.at[pl.ds(NCH, NCH)], hms.at[d])

    core_q.wait_send()
    core_l.wait_send()
    others = pl.ds(1, NX * NZ - 1)
    wait_all(all_q.at[others], qss)
    wait_all(all_l.at[others], lss)
    wait_all(all_t.at[others], tss)
    wait_all(all_l.at[others], lsr)
    lse_l, t_l = merge_l(*(all_l[:, i, :] for i in range(2)))
    for j in range(NCH):
        l_fac[j] = jnp.exp(l_tops[j] - lse_l)
    wait_all(all_q.at[others], qsr)
    total_q, mass_q = (log_add(all_q[:, i, :]) for i in range(2))
    log_norm = jnp.log(1.0 + jnp.exp(mass_q - total_q))
    norm_out[...] = log_norm
    m_fac[...] = jnp.exp(shift - total_q)
    wait_all(all_t.at[others], tsr)
    nll[...] = log_norm - jnp.log(
        jnp.maximum(jnp.exp(t_l - lse_l), FLOOR) + jnp.exp(log_add(all_t[:, 0, :]) - total_q)
    )


def finish(el, mp_buf, l_fac, m_fac, norm_out, nll_in, out, nll, buf, sem):
    rows_i = lax.broadcasted_iota(jnp.int32, (Q, Q), 0)
    cols_i = lax.broadcasted_iota(jnp.int32, (Q, Q), 1)

    def to_col(row):
        return jnp.sum(jnp.where(rows_i == cols_i, row, 0.0), axis=1, keepdims=True)

    copies = [pltpu.make_async_copy(nll_in, nll, sem.at[NCH])]
    copies[0].start()
    norm_col, m_col = to_col(norm_out[...]), to_col(m_fac[...])
    for j in range(NCH):
        at = slice((j % 2) * CW, (j % 2 + 1) * CW)
        mapped = mp_buf[j // 2, :, at]
        buf[:, j * CW : (j + 1) * CW] = (
            jnp.log(jnp.maximum(el[j] * to_col(l_fac[j]), FLOOR) + mapped * m_col) - norm_col
        )
        cols = pl.ds(j * CW, CW)
        copies.append(pltpu.make_async_copy(buf.at[:, cols], out.at[:, cols], sem.at[j]))
        copies[-1].start()
    for cp in copies:
        cp.wait()


def on_device(
    hidden, norm_gain, head_weights, pair_source, pair_target, pair_count, pair_weight, next_token
):
    hbm = pl.BlockSpec(memory_space=pltpu.HBM)
    vmem = pl.BlockSpec(memory_space=pltpu.VMEM)
    dma = pltpu.SemaphoreType.DMA
    f32, bf16 = jnp.float32, jnp.bfloat16
    parts = pl.pallas_call(
        kernel,
        out_shape=(
            pltpu.VMEM((NCH, Q, CW), f32),
            pltpu.VMEM((NB, Q, BLOCK), f32),
            pltpu.VMEM((NCH, 1, Q), f32),
            pltpu.VMEM((1, Q), f32),
            pltpu.VMEM((1, Q), f32),
            pltpu.VMEM((1, Q), f32),
        ),
        in_specs=[pl.BlockSpec(memory_space=pl.ANY)] * 8,
        out_specs=(vmem,) * 6,
        scratch_shapes=[
            pltpu.SMEM((4,), jnp.int32),
            pltpu.SMEM((4,), jnp.int32),
            pltpu.SMEM((1,), jnp.int32),
            pltpu.VMEM((Q,), jnp.int32),
            pltpu.VMEM((4, Q, FEAT), bf16),
            pltpu.VMEM((8 * Q, FEAT), bf16),
            pltpu.VMEM((1, FEAT), bf16),
            pltpu.VMEM((NCH, FEAT, CW), bf16),
            pltpu.VMEM((4, BLOCK, BLOCK), bf16),
            pltpu.VMEM((NCH, 3, Q, CW), jnp.int16),
            pltpu.VMEM((NCH, 3, 2, Q), f32),
            pltpu.VMEM((2, 3, Q, CW), f32),
            pltpu.VMEM((NCH, 3, Q, CW), jnp.int16),
            pltpu.VMEM((NCH, 3, 2, Q), f32),
            pltpu.VMEM((NCH, Q, CW), f32),
            pltpu.VMEM((1, Q), f32),
            pltpu.VMEM((2, Q, CW), f32),
            pltpu.VMEM((3 * NCH, Q, CW), bf16),
            pltpu.VMEM((3 * NCH, 1, Q), f32),
            pltpu.VMEM((NCH, 1, Q), f32),
            pltpu.VMEM((NCH, 1, Q), f32),
            pltpu.VMEM((NCH, 1, Q), f32),
            pltpu.VMEM((NCH, 1, Q), f32),
            pltpu.VMEM((3, Q), f32),
            pltpu.VMEM((3, Q), f32),
            pltpu.VMEM((NX * NZ, 2, Q), f32),
            pltpu.VMEM((NX * NZ, 1, Q), f32),
            pltpu.VMEM((2, Q), f32),
            pltpu.VMEM((2, Q), f32),
            pltpu.VMEM((NX * NZ, 2, Q), f32),
            dma((7,)),
            dma((4,)),
            dma((NCH,)),
            dma(()),
            dma((NCH + 2,)),
            dma(()),
            dma((NCH,)),
            dma((2,)),
            dma((2,)),
            dma((2,)),
            dma((2,)),
            dma((4,)),
            dma(()),
            dma(()),
            dma(()),
            dma(()),
            dma(()),
            dma(()),
        ],
        compiler_params=pltpu.CompilerParams(
            collective_id=0, has_side_effects=True, vmem_limit_bytes=40 * 2**20
        ),
        cost_estimate=pl.CostEstimate(
            flops=4 * 4 * Q * FEAT * NB * BLOCK, bytes_accessed=12 * 2**20, transcendentals=10**6
        ),
        name="ensemble",
    )(
        *(a if a.shape == (1,) else pltpu.with_memory_space_constraint(a, pltpu.HBM) for a in (
            hidden, norm_gain, head_weights, pair_source, pair_target, pair_count, pair_weight,
            next_token,
        ))
    )
    ensemble, nll = pl.pallas_call(
        finish,
        out_shape=(
            jax.ShapeDtypeStruct((Q, NB * BLOCK), f32),
            jax.ShapeDtypeStruct((1, Q), f32),
        ),
        in_specs=[vmem] * 6,
        out_specs=(pl.BlockSpec(memory_space=pl.ANY),) * 2,
        scratch_shapes=[pltpu.VMEM((Q, NB * BLOCK), f32), dma((NCH + 2,))],
        compiler_params=pltpu.CompilerParams(vmem_limit_bytes=32 * 2**20),
        name="finish",
    )(*parts)
    return ensemble, nll.reshape(Q)


def solution(mesh):
    in_specs = (
        P("mp", None, "rows"),
        P("mp", "rows"),
        P("mp", "rows", "vocab"),
        P("vocab"),
        P("vocab"),
        P("vocab"),
        P("vocab", None, None),
        P(("mp", "rows")),
    )
    out_specs = (P(("mp", "rows"), "vocab"), P(("mp", "rows")))
    return jax.shard_map(
        on_device, mesh=mesh, in_specs=in_specs, out_specs=out_specs, check_vma=False
    )
```
